256 devices in a mesh: row: 16 (over x_hi, y, core), col: 16 (over x_lo, z).
Axes of the slice: x: 4 (x_hi: 2, x_lo: 2; x = x_hi * 2 + x_lo), y: 4, z: 8, core: 2. Of those that a mesh axis runs over, the one named last changes fastest.
Arguments:
- amplitudes: bfloat16 [2048, 8, 2048], P('row', None, 'col'), may hold values from -6 to 6
- factors: bfloat16 [16, 2048, 2048], P(None, 'row', 'col'), may hold values from -0.0625 to 0.0625
- virt_irrep: int32 [32], replicated, may hold values from 0 to 1
- occupied_symmetry_label: int32 [200], replicated, may hold values from 0 to 1
- pair_index: int32 [8, 2], replicated, may hold values from 0 to 199
Outputs:
- ladder: bfloat16 [2048, 8, 2048], P('row', None, 'col')
The draws below stay inside these ranges and needn't reach their ends.
All inputs are finite; a program needn't handle non-finite values.
Results may differ from the reference program's by a relative error of at most 0.0049.
Values may be sent and summed in bfloat16 or wider, within the bound.
A program may use at most 64 MiB of HBM per device.

```python
import jax
import jax.numpy as jnp
from jax import lax

NV = 2048
VB = 64
NOCC = 200
PAIRS = 8
QB = 16
NBLK = 32


def set_ends(drawn, stream_key, least, high):
    index_at = [jax.random.randint(jax.random.fold_in(stream_key, axis), (), 0, length) for axis, length in enumerate(drawn.shape)]
    longest = drawn.shape.index(max(drawn.shape))
    next_to = index_at[:longest] + [(index_at[longest] + 1) % drawn.shape[longest]] + index_at[longest + 1:]
    return drawn.at[tuple(index_at)].set(least).at[tuple(next_to)].set(high)


def block_scale(stream_key, extent, pieces, least, largest):
    def one(dim, parts):
        steps = jax.random.uniform(jax.random.fold_in(jax.random.fold_in(stream_key, 6), dim), (parts,), jnp.float32, least / len(pieces), largest / len(pieces))
        return jnp.repeat(jnp.exp(steps), extent[dim] // parts).reshape((-1,) + (1,) * (len(extent) - dim - 1))

    level = one(*pieces[0])
    for cut in pieces[1:]:
        level = level * one(*cut)
    return level


def normal_values(stream_key, shape, deviation, limit, cuts=(), held_as=jnp.bfloat16):
    result = deviation * jax.random.normal(stream_key, shape, jnp.float32)
    if cuts:
        result = result * block_scale(stream_key, shape, cuts, -0.22, 0.18)
    return jnp.clip(result, -limit, limit).astype(held_as)


def setup_inputs(seed: int = 0) -> dict:
    key_of = jax.random.split(jax.random.key(seed), 6)
    amplitudes = normal_values(key_of[0], (NV, PAIRS, NV), 1.0, 6.0, ((0, 16), (2, 16)))
    factors = normal_values(key_of[1], (QB, NV, NV), (NV * 4) ** -0.5, 0.0625, ((1, 16), (2, 16)))
    virt_irrep = set_ends(jax.random.randint(key_of[2], (NBLK,), 0, 2), jax.random.fold_in(key_of[2], 1), 0, 1).astype(jnp.int32)
    occupied_symmetry_label = set_ends(jax.random.randint(key_of[3], (NOCC,), 0, 2), jax.random.fold_in(key_of[3], 1), 0, 1).astype(jnp.int32)
    pair_index = set_ends(jax.random.randint(key_of[4], (PAIRS, 2), 0, NOCC), jax.random.fold_in(key_of[4], 1), 0, NOCC - 1).astype(jnp.int32)
    return {"amplitudes": amplitudes, "factors": factors, "virt_irrep": virt_irrep, "occupied_symmetry_label": occupied_symmetry_label, "pair_index": pair_index}


def labels(virt_irrep, occupied_symmetry_label, pair_index):
    blocks = jnp.arange(NV, dtype=jnp.int32) // VB
    lab_v = virt_irrep[blocks]
    lab_p = occupied_symmetry_label[pair_index[:, 0]] + occupied_symmetry_label[pair_index[:, 1]]
    grand_total_sum = lab_v[:, None, None] + lab_p[None, :, None] + lab_v[None, None, :]
    return (grand_total_sum % 2 == 0).astype(jnp.float32)


def reference(amplitudes, factors, virt_irrep, occupied_symmetry_label, pair_index):
    allowed = labels(virt_irrep, occupied_symmetry_label, pair_index)
    masked_terms = (amplitudes.astype(jnp.float32) * allowed).astype(jnp.bfloat16).astype(jnp.float32)

    def step(grand_total_sum, factor_q):
        fitted_factor_matrix = factor_q.astype(jnp.float32)
        half_span = jnp.einsum("jmq,qk->jmk", masked_terms, fitted_factor_matrix).astype(jnp.bfloat16).astype(jnp.float32)
        return grand_total_sum + jnp.einsum("sg,srl->grl", fitted_factor_matrix, half_span), None

    start = jnp.zeros((NV, PAIRS, NV), jnp.float32)
    full, _ = lax.scan(step, start, factors)
    return (allowed * full).astype(jnp.bfloat16)
```

```python
import functools

import jax
import jax.numpy as jnp
from jax import lax
from jax.experimental import pallas as pl
from jax.experimental.pallas import tpu as pltpu
from jax.sharding import PartitionSpec as P

NV = 2048
VB = 64
MESH = pl.DeviceIdType.MESH
N_SEMS = 112


def lookup(index_entries, table):
    places = jnp.arange(table.shape[0], dtype=jnp.int32)
    hits = index_entries[..., None] == places
    return jnp.sum(jnp.where(hits, table, 0), axis=-1)


def kernel(
    t_ref, ft_ref, f_ref, out_ref,
    t_all, fca, fdb, ht, rp, ra1, ra2, rb1, rb2, rc1, rc2, fin, fin_in,
    send, recv,
):
    row, col = lax.axis_index("row"), lax.axis_index("col")
    xh, y, k = row // 8, (row // 2) % 4, row % 2
    xl, z = col // 8, col % 8
    x = xh * 2 + xl

    def dev(x_to, y_to, z_to, k_to):
        return {"row": (x_to // 2) * 8 + y_to * 2 + k_to, "col": (x_to % 2) * 8 + z_to}

    def wrap(v, n):
        return lax.rem(v + n, n)

    xs = {s: wrap(x + s, 4) for s in (-1, 0, 1, 2)}
    ys = {s: wrap(y + s, 4) for s in (-1, 0, 1, 2)}
    zs = {s: wrap(z + s, 8) for s in range(-4, 5)}
    near = {
        "x": {s: dev(xs[s], y, z, k) for s in (-1, 1)},
        "y": {s: dev(x, ys[s], z, k) for s in (-1, 1)},
        "z": {s: dev(x, y, zs[s], k) for s in (-1, 1)},
    }
    sibling = dev(x, y, z, 1 - k)
    partner = dev(xh * 2 + k, y, z, xl)
    swapped = xl != k

    count = [0]
    pending = []

    def put(src, dst, device):
        number = count[0]
        count[0] += 1
        copy = pltpu.make_async_remote_copy(
            src_ref=src, dst_ref=dst, send_sem=send.at[number], recv_sem=recv.at[number],
            device_id=device, device_id_type=MESH,
        )
        copy.start()
        pending.append(copy)
        return copy

    barrier = pltpu.get_barrier_semaphore()
    for target in [*near["x"].values(), *near["y"].values(), *near["z"].values(), sibling]:
        pl.semaphore_signal(barrier, inc=1, device_id=target, device_id_type=MESH)

    @pl.when(swapped)
    def _():
        pl.semaphore_signal(barrier, inc=1, device_id=partner, device_id_type=MESH)
        pl.semaphore_wait(barrier, 8)

    @pl.when(jnp.logical_not(swapped))
    def _():
        pl.semaphore_wait(barrier, 7)

    moves = []
    for src, dst in (
        (t_ref, t_all.at[col]),
        (ft_ref, fdb.at[xh, y, k]),
        (f_ref, fca.at[col]),
    ):
        number = count[0]
        count[0] += 1
        far = pltpu.make_async_remote_copy(
            src_ref=src, dst_ref=dst, send_sem=send.at[number], recv_sem=recv.at[number],
            device_id=partner, device_id_type=MESH,
        )
        near_copy = pltpu.make_async_copy(src, dst, recv.at[number])
        moves.append((far, near_copy))

        @pl.when(swapped)
        def _():
            far.start()

        @pl.when(jnp.logical_not(swapped))
        def _():
            near_copy.start()

    def own_here(i):
        far, near_copy = moves[i]

        @pl.when(swapped)
        def _():
            far.wait_recv()

        @pl.when(jnp.logical_not(swapped))
        def _():
            near_copy.wait()

    ring_wait = {}
    side_wait = {"t": [], "f": []}

    def part(name, shard, half):
        buf = t_all if name == "t" else fca
        at = k * 8 + shard
        rows = buf.shape[1]
        if half is None:
            return buf.at[at]
        return buf.at[at, pl.ds(half * (rows // 2), rows // 2)]

    def ring_send(name, step):
        for sign in (1, -1):
            shard = zs[-sign * (step - 1)]
            piece = part(name, shard, None if step < 4 else (1 - sign) // 2)
            ring_wait[name, step, sign] = put(piece, piece, near["z"][sign])

    def side_send(name, shard, half=None):
        piece = part(name, shard, half)
        side_wait[name].append(put(piece, piece, sibling))

    def ring_step(name, step):
        for sign in (1, -1):
            ring_wait[name, step, sign].wait_recv()
        if step < 4:
            ring_send(name, step + 1)
            for sign in (1, -1):
                side_send(name, zs[-sign * step])
        else:
            side_send(name, zs[4])

    def cell(half, u, v):
        a, b = (u, v) if half == 0 else (v, u)
        return a // 2, b, a % 2

    axes = {0: ("x", "y", xs, ys), 1: ("y", "x", ys, xs)}

    def shard_of(half, u, v, quarter=None):
        start = half * 8 if quarter is None else half * 8 + quarter * 4
        return fdb.at[(*cell(half, u, v), pl.ds(start, 8 if quarter is None else 4))]

    first, second, across, across2 = {}, {}, {}, {}

    def along_v(half, i):
        u_axis, v_axis, us, vs = axes[half]
        piece = shard_of(half, us[(0, -1, 1, 2)[i]], vs[0])
        for sign in (1, -1):
            across[half, i, sign] = put(piece, piece, near[v_axis][sign])

    def plane_start(half):
        u_axis, _, us, vs = axes[half]
        piece = shard_of(half, us[0], vs[0])
        for sign in (1, -1):
            first[half, sign] = put(piece, piece, near[u_axis][sign])

    def plane_first(half):
        u_axis, _, us, vs = axes[half]
        for sign in (1, -1):
            first[half, sign].wait_recv()
            piece = shard_of(half, us[-sign], vs[0], (1 - sign) // 2)
            second[half, sign] = put(piece, piece, near[u_axis][sign])
        along_v(half, 1)
        along_v(half, 2)

    def plane_second(half):
        for sign in (1, -1):
            second[half, sign].wait_recv()
        along_v(half, 3)

    def plane_across(half, i):
        _, v_axis, us, vs = axes[half]
        for sign in (1, -1):
            across[half, i, sign].wait_recv()
            piece = shard_of(half, us[(0, -1, 1, 2)[i]], vs[-sign], (1 - sign) // 2)
            across2[half, i, sign] = put(piece, piece, near[v_axis][sign])

    def both(step, *args):
        for half in (0, 1):
            step(half, *args)

    own_here(0)
    ring_send("t", 1)
    side_send("t", zs[0])
    own_here(1)
    both(plane_start)
    both(along_v, 0)
    ring_step("t", 1)
    own_here(2)
    ring_send("f", 1)
    side_send("f", zs[0])
    ring_step("t", 2)
    both(plane_first)
    ring_step("t", 3)
    both(plane_across, 0)
    ring_step("t", 4)
    both(plane_second)
    ring_step("f", 1)
    both(plane_across, 1)
    both(plane_across, 2)
    ring_step("f", 2)
    both(plane_across, 3)
    for copy in side_wait["t"]:
        copy.wait_recv()

    def stage1(half):
        for i in range(4):
            for sign in (1, -1):
                across2[half, i, sign].wait_recv()

        def body(n, _):
            lhs = jnp.concatenate(
                [
                    fdb[r // 8, (r // 2) % 4, r % 2, half * 8 : half * 8 + 8].reshape(1024, 128)
                    for r in range(16)
                ],
                axis=1,
            )
            rhs = t_all[:, :, pl.ds(pl.multiple_of(n * 256, 256), 256)].reshape(2048, 256)
            out = jnp.dot(lhs, rhs, preferred_element_type=jnp.float32).astype(jnp.bfloat16)
            for i in range(2):
                rows = pl.ds(pl.multiple_of(n * 256 + i * 128, 128), 128)
                for j in range(8):
                    at = (half * 8 + j) * 128
                    ht[rows, at : at + 128] = out[j * 128 : j * 128 + 128, i * 128 : i * 128 + 128]
            return 0

        lax.fori_loop(0, 4, body, 0)

    stage1(0)
    ring_step("f", 3)
    stage1(1)
    ring_step("f", 4)
    for copy in side_wait["f"]:
        copy.wait_recv()

    def stage2(lo, hi):
        def body(n, _):
            y_to = wrap(y + 2 + n // 2, 4)
            xh_to = lax.rem(n, 2)
            r = xh_to * 8 + y_to * 2
            rhs = jnp.concatenate(
                [fca[r].reshape(2048, 128), fca[r + 1].reshape(2048, 128)], axis=1
            )
            out = jnp.dot(ht[...], rhs, preferred_element_type=jnp.float32).astype(jnp.bfloat16)
            rp[xh_to, y_to, 0] = out[:, :128]
            rp[xh_to, y_to, 1] = out[:, 128:]
            return 0

        lax.fori_loop(lo, hi, body, 0)

    def strip(half, v, start, size):
        if half == 0:
            return (slice(None), v, slice(None), pl.ds(start, size))
        return (v // 2, slice(None), v % 2, pl.ds(start, size))

    sums1, sums2, last1, last2 = {}, {}, {}, {}
    got1, got2 = {0: ra1, 1: rb1}, {0: ra2, 1: rb2}
    scatter = {0: ("y", "x", ys, xs), 1: ("x", "y", xs, ys)}

    def slot(sign):
        return (1 - sign) // 2

    def quarter(half, sign):
        return half * 512 + slot(sign) * 256

    def one(half, u):
        return (u // 2, y, u % 2) if half == 0 else (x // 2, u, x % 2)

    def f32(v):
        return v.astype(jnp.float32)

    def sum_first(half):
        axis, _, vs, _ = scatter[half]
        for sign in (1, -1):
            src = rp.at[strip(half, vs[2], quarter(half, sign), 256)]
            sums1[half, sign] = put(src, got1[half].at[slot(sign)], near[axis][sign])

    def sum_second(half):
        axis, _, vs, _ = scatter[half]
        for sign in (1, -1):
            sums1[half, sign].wait_recv()
            at = strip(half, vs[sign], quarter(half, sign), 256)
            rp[at] = (f32(rp[at]) + f32(got1[half][slot(sign)])).astype(jnp.bfloat16)
            src = rp.at[strip(half, vs[sign], half * 512, 512)]
            sums2[half, sign] = put(src, got2[half].at[slot(sign)], near[axis][sign])

    def sum_third(half):
        _, axis, vs, us = scatter[half]
        for sign in (1, -1):
            sums2[half, sign].wait_recv()
        at = strip(half, vs[0], half * 512, 512)
        rp[at] = (f32(rp[at]) + f32(got2[half][0]) + f32(got2[half][1])).astype(jnp.bfloat16)
        for sign in (1, -1):
            src = rp.at[(*one(half, us[2]), pl.ds(quarter(half, sign), 256))]
            last1[half, sign] = put(src, rc1.at[half, slot(sign)], near[axis][sign])

    def sum_fourth(half):
        _, axis, _, us = scatter[half]
        for sign in (1, -1):
            last1[half, sign].wait_recv()
            at = (*one(half, us[sign]), pl.ds(quarter(half, sign), 256))
            rp[at] = (f32(rp[at]) + f32(rc1[half, slot(sign)])).astype(jnp.bfloat16)
            src = rp.at[(*one(half, us[sign]), pl.ds(half * 512, 512))]
            last2[half, sign] = put(src, rc2.at[half, slot(sign)], near[axis][sign])

    def sum_last(half):
        _, _, _, us = scatter[half]
        for sign in (1, -1):
            last2[half, sign].wait_recv()
        rows = pl.ds(half * 512, 512)
        mine = f32(rp[(*one(half, us[0]), rows)])
        fin[rows, :] = (mine + f32(rc2[half, 0]) + f32(rc2[half, 1])).astype(jnp.bfloat16)

    stage2(0, 2)
    sum_first(0)
    stage2(2, 8)
    sum_first(1)
    both(sum_second)
    both(sum_third)
    both(sum_fourth)
    both(sum_last)

    number = count[0]
    back = pltpu.make_async_remote_copy(
        src_ref=fin, dst_ref=fin_in, send_sem=send.at[number], recv_sem=recv.at[number],
        device_id=partner, device_id_type=MESH,
    )

    @pl.when(swapped)
    def _():
        back.start()
        back.wait()
        out_ref[...] = fin_in[...]
        for far, _ in moves:
            far.wait_send()

    @pl.when(jnp.logical_not(swapped))
    def _():
        out_ref[...] = fin[...]

    for copy in pending:
        copy.wait_send()


def ladder(t, ft, f):
    bf16 = jnp.bfloat16
    hbm, vmem = pl.BlockSpec(memory_space=pl.ANY), pl.BlockSpec(memory_space=pltpu.VMEM)
    return pl.pallas_call(
        kernel,
        out_shape=jax.ShapeDtypeStruct((1024, 128), bf16),
        in_specs=[hbm, hbm, hbm],
        out_specs=vmem,
        scratch_shapes=[
            pltpu.VMEM((16, 128, 1024), bf16),
            pltpu.VMEM((16, 16, 128, 128), bf16),
            pltpu.VMEM((2, 4, 2, 16, 128, 128), bf16),
            pltpu.VMEM((1024, 2048), bf16),
            pltpu.VMEM((2, 4, 2, 1024, 128), bf16),
            pltpu.VMEM((2, 2, 2, 256, 128), bf16),
            pltpu.VMEM((2, 2, 2, 512, 128), bf16),
            pltpu.VMEM((2, 4, 256, 128), bf16),
            pltpu.VMEM((2, 4, 512, 128), bf16),
            pltpu.VMEM((2, 2, 256, 128), bf16),
            pltpu.VMEM((2, 2, 512, 128), bf16),
            pltpu.VMEM((1024, 128), bf16),
            pltpu.VMEM((1024, 128), bf16),
            pltpu.SemaphoreType.DMA((N_SEMS,)),
            pltpu.SemaphoreType.DMA((N_SEMS,)),
        ],
        compiler_params=pltpu.CompilerParams(
            collective_id=0, has_side_effects=True, vmem_limit_bytes=56 * 1024 * 1024
        ),
    )(t, ft, f)


def on_device(amplitudes, factors, virt_irrep, occupied_symmetry_label, pair_index):
    rows, pairs, width = amplitudes.shape
    row_start = lax.axis_index("row") * rows
    col_start = lax.axis_index("col") * width
    row_ids = (row_start + jnp.arange(rows, dtype=jnp.int32)) // VB
    col_ids = (col_start + jnp.arange(width, dtype=jnp.int32)) // VB
    lab_rows = lookup(row_ids, virt_irrep)
    lab_cols = lookup(col_ids, virt_irrep)
    lab_pair = lookup(pair_index[:, 0], occupied_symmetry_label) + lookup(
        pair_index[:, 1], occupied_symmetry_label
    )
    parity = lab_rows[:, None, None] + lab_pair[None, :, None] + lab_cols[None, None, :]
    allowed = parity % 2 == 0
    zero = jnp.zeros((), jnp.bfloat16)
    masked = jnp.where(allowed, amplitudes, zero)
    t = masked.transpose(2, 1, 0).reshape(width, pairs * rows)
    full = ladder(t, factors.transpose(0, 2, 1), factors)
    full = full.reshape(pairs, width, rows).transpose(2, 0, 1)
    return jnp.where(allowed, full, zero)


def solution(mesh):
    in_specs = (P("row", None, "col"), P(None, "row", "col"), P(), P(), P())
    out_specs = P("row", None, "col")
    return jax.shard_map(
        on_device, mesh=mesh, in_specs=in_specs, out_specs=out_specs, check_vma=False
    )
```

```python
import jax
import jax.numpy as jnp
from jax import lax
from jax.experimental import pallas as pl
from jax.experimental.pallas import tpu as pltpu
from jax.sharding import PartitionSpec as P

VB = 64
MESH = pl.DeviceIdType.MESH
N_SEMS = 160


def kernel(
    virt, occ, pair, t_ref, ft_ref, f_ref, out_ref,
    t_own, t_all, fca, fdb, ht, rp, ra1, ra2, rb1, rb2, rc1, rc2, fin, fin_in,
    send, recv,
):
    row, col = lax.axis_index("row"), lax.axis_index("col")
    xh, y, k = row // 8, (row // 2) % 4, row % 2
    xl, z = col // 8, col % 8
    x = xh * 2 + xl

    def dev(x_to, y_to, z_to, k_to):
        return {"row": (x_to // 2) * 8 + y_to * 2 + k_to, "col": (x_to % 2) * 8 + z_to}

    def wrap(v, n):
        return lax.rem(v + n, n)

    xs = {s: wrap(x + s, 4) for s in (-1, 0, 1, 2)}
    ys = {s: wrap(y + s, 4) for s in (-1, 0, 1, 2)}
    zs = {s: wrap(z + s, 8) for s in range(-4, 5)}
    near = {
        "x": {s: dev(xs[s], y, z, k) for s in (-1, 1)},
        "y": {s: dev(x, ys[s], z, k) for s in (-1, 1)},
        "z": {s: dev(x, y, zs[s], k) for s in (-1, 1)},
    }
    sibling = dev(x, y, z, 1 - k)
    partner = dev(xh * 2 + k, y, z, xl)
    swapped = xl != k
    home = xl == k

    count = [0]
    pending = []

    def when(condition, action):
        if condition is None:
            action()
        else:
            pl.when(condition)(action)

    def put(src, dst, device, condition=None):
        number = count[0]
        count[0] += 1
        copy = pltpu.make_async_remote_copy(
            src_ref=src, dst_ref=dst, send_sem=send.at[number], recv_sem=recv.at[number],
            device_id=device, device_id_type=MESH,
        )
        when(condition, copy.start)
        pending.append((condition, copy))
        return copy

    def sign_of(label):
        return (1 - 2 * lax.rem(label, 2)).astype(jnp.float32)

    def two(block):
        low = lax.broadcasted_iota(jnp.int32, (1, 128), 1) < VB
        return jnp.where(low, sign_of(virt[2 * block]), sign_of(virt[2 * block + 1]))

    def two_rows(block):
        low = lax.broadcasted_iota(jnp.int32, (128, 1), 0) < VB
        return jnp.where(low, sign_of(virt[2 * block]), sign_of(virt[2 * block + 1]))

    pair_sign = [sign_of(occ[pair[2 * p]] + occ[pair[2 * p + 1]]) for p in range(8)]

    def mask(p):
        return 0.5 + 0.5 * (two_rows(col) * (two(row) * pair_sign[p]))

    barrier = pltpu.get_barrier_semaphore()
    for target in [*near["x"].values(), *near["y"].values(), *near["z"].values(), sibling]:
        pl.semaphore_signal(barrier, inc=1, device_id=target, device_id_type=MESH)

    for p in range(8):
        at = slice(p * 128, p * 128 + 128)
        t_own[:, at] = (t_ref[:, at].astype(jnp.float32) * mask(p)).astype(jnp.bfloat16)

    @pl.when(swapped)
    def _():
        pl.semaphore_signal(barrier, inc=1, device_id=partner, device_id_type=MESH)
        pl.semaphore_wait(barrier, 8)

    @pl.when(jnp.logical_not(swapped))
    def _():
        pl.semaphore_wait(barrier, 7)

    moves = []
    for src, dst in ((t_own, t_all.at[col]), (f_ref, fca.at[col])):
        number = count[0]
        count[0] += 1
        far = pltpu.make_async_remote_copy(
            src_ref=src, dst_ref=dst, send_sem=send.at[number], recv_sem=recv.at[number],
            device_id=partner, device_id_type=MESH,
        )
        near_copy = pltpu.make_async_copy(src, dst, recv.at[number])
        moves.append((far, near_copy))

    def own_start(i):
        far, near_copy = moves[i]

        @pl.when(swapped)
        def _():
            far.start()

        @pl.when(jnp.logical_not(swapped))
        def _():
            near_copy.start()

    def own_here(i):
        far, near_copy = moves[i]

        @pl.when(swapped)
        def _():
            far.wait_recv()

        @pl.when(jnp.logical_not(swapped))
        def _():
            near_copy.wait()

    ring_wait = {}
    side_wait = {}

    def part(name, shard, half):
        buf = t_all if name == "t" else fca
        at = k * 8 + shard
        rows = buf.shape[1]
        if half is None:
            return buf.at[at]
        return buf.at[at, pl.ds(half * (rows // 2), rows // 2)]

    def side_send(name, step):
        for sign in (1, -1) if step % 4 else (1,):
            piece = part(name, zs[-sign * step], None)
            side_wait[name, step, sign] = put(piece, piece, sibling)

    def side_done(name, step):
        for sign in (1, -1) if step % 4 else (1,):
            side_wait[name, step, sign].wait_recv()

    def t_send(step):
        for sign in (1, -1):
            piece = part("t", zs[-sign * (step - 1)], None if step < 4 else (1 - sign) // 2)
            ring_wait["t", step, sign] = put(piece, piece, near["z"][sign])

    def t_step(step):
        for sign in (1, -1):
            ring_wait["t", step, sign].wait_recv()
        if step < 4:
            t_send(step + 1)
        side_send("t", step)

    def t_done():
        for step in range(5):
            side_done("t", step)

    def f_send(step, half):
        for sign in (1, -1):
            if step < 4 or half == (1 - sign) // 2:
                piece = part("f", zs[-sign * (step - 1)], half)
                ring_wait["f", step, sign, half] = put(piece, piece, near["z"][sign])

    def f_step(step, half):
        for sign in (1, -1):
            if step < 4 or half == (1 - sign) // 2:
                ring_wait["f", step, sign, half].wait_recv()
        if step < 4:
            f_send(step + 1, half)
        if half == 1:
            side_send("f", step)

    def unit(xh_of, y_of, start, size):
        return fdb.at[xh_of, y_of, :, pl.ds(start, size)]

    def both_ways(piece, axis, condition=None):
        return {sign: put(piece, piece, near[axis][sign], condition) for sign in (1, -1)}

    lines = [jnp.where(home, xh, xs[-1] // 2), jnp.where(home, 1 - xh, xs[1] // 2)]
    sides = {1: xs[-1] // 2, -1: xs[1] // 2}
    moved = {}

    def wait(key, condition=None):
        for sign in (1, -1):
            when(condition, moved[key][sign].wait_recv)

    def a_start(s):
        own = unit(xh, y, 4 * s, 4)
        moved["ax", s] = both_ways(own, "x", home)

    def a_along(s, i, condition=None):
        piece = unit(lines[i], y, 4 * s, 4)
        return both_ways(piece, "y", condition)

    def b_start(s):
        own = unit(xh, y, 8 + 4 * s, 4)
        moved["by", s] = both_ways(own, "y", home)
        b_along(s, 0)

    def b_along(s, j):
        piece = unit(xh, ys[(0, -1, 1, 2)[j]], 8 + 4 * s, 4)
        moved["bx", s, j] = both_ways(piece, "x", home)

    def a_x(s):
        wait(("ax", s), swapped)
        moved["ax2", s] = {
            sign: put(piece, piece, near["x"][sign], swapped)
            for sign in (1, -1)
            for piece in [unit(sides[sign], y, 4 * s + 1 - sign, 2)]
        }
        moved["ay", s, 0] = a_along(s, 0)

    def a_x2(s):
        wait(("ax2", s), home)
        moved["ay", s, 1] = a_along(s, 1)

    def a_y(s, i):
        wait(("ay", s, i))
        moved["ay2", s, i] = {
            sign: put(piece, piece, near["y"][sign])
            for sign in (1, -1)
            for piece in [unit(lines[i], ys[-sign], 4 * s + 1 - sign, 2)]
        }

    def b_y(s):
        wait(("by", s), home)
        moved["by2", s] = {
            sign: put(piece, piece, near["y"][sign], home)
            for sign in (1, -1)
            for piece in [unit(xh, ys[-sign], 8 + 4 * s + 1 - sign, 2)]
        }
        b_along(s, 1)
        b_along(s, 2)

    def b_y2(s):
        wait(("by2", s), home)
        b_along(s, 3)

    def b_x(s, j):
        wait(("bx", s, j), swapped)
        moved["bx2", s, j] = {
            sign: put(piece, piece, near["x"][sign], swapped)
            for sign in (1, -1)
            for piece in [unit(sides[sign], ys[(0, -1, 1, 2)[j]], 8 + 4 * s + 1 - sign, 2)]
        }

    def a_done(s):
        for i in (0, 1):
            wait(("ay2", s, i))

    def b_done(s):
        for j in range(4):
            wait(("bx2", s, j), home)

    given = put(ft_ref, fdb.at[xh, y, k], sibling, swapped)
    kept = pltpu.make_async_copy(ft_ref, fdb.at[xh, y, k], send.at[N_SEMS - 1])
    pl.when(home)(kept.start)

    def plane_own():
        pl.when(home)(given.wait_recv)
        pl.when(home)(kept.wait)

    def stage1(first_q):
        def body(n, _):
            lhs = jnp.concatenate(
                [
                    fdb[r // 8, (r // 2) % 4, r % 2, first_q : first_q + 4].reshape(512, 128)
                    for r in range(16)
                ],
                axis=1,
            )
            rhs = t_all[:, :, pl.ds(pl.multiple_of(n * 256, 256), 256)].reshape(2048, 256)
            out = jnp.dot(lhs, rhs, preferred_element_type=jnp.float32).astype(jnp.bfloat16)
            for i in range(2):
                rows = pl.ds(pl.multiple_of(n * 256 + i * 128, 128), 128)
                for j in range(4):
                    at = (first_q + j) * 128
                    ht[rows, at : at + 128] = out[j * 128 : j * 128 + 128, i * 128 : i * 128 + 128]
            return 0

        lax.fori_loop(0, 4, body, 0)

    def stage2(lo, hi):
        for step in sorted({(n + 1) // 2 for n in range(lo, hi)}):
            side_done("f", step)

        def body(n, _):
            away = (n + 1) // 2
            shard = wrap(z + jnp.where(lax.rem(n, 2) == 1, away, 8 - away), 8)
            rhs = jnp.concatenate(
                [fca[shard].reshape(2048, 128), fca[8 + shard].reshape(2048, 128)], axis=1
            )
            out = jnp.dot(ht[...], rhs, preferred_element_type=jnp.float32).astype(jnp.bfloat16)
            rp[0, shard // 2, lax.rem(shard, 2)] = out[:, :128]
            rp[1, shard // 2, lax.rem(shard, 2)] = out[:, 128:]
            return 0

        lax.fori_loop(lo, hi, body, 0)

    def strip(half, v, start, size):
        if half == 0:
            return (slice(None), v, slice(None), pl.ds(start, size))
        return (v // 2, slice(None), v % 2, pl.ds(start, size))

    sums1, sums2, last1, last2, alone1, alone2, back = {}, {}, {}, {}, {}, {}, {}
    got1, got2 = {0: ra1, 1: rb1}, {0: ra2, 1: rb2}
    scatter = {0: ("y", "x", ys, xs), 1: ("x", "y", xs, ys)}

    def slot(sign):
        return (1 - sign) // 2

    def quarter(half, sign):
        return half * 512 + slot(sign) * 256

    def one(half, u):
        return (u // 2, y, u % 2) if half == 0 else (x // 2, u, x % 2)

    def f32(v):
        return v.astype(jnp.float32)

    def sum_first(half):
        axis, _, vs, _ = scatter[half]
        for sign in (1, -1):
            src = rp.at[strip(half, vs[2], quarter(half, sign), 256)]
            sums1[half, sign] = put(src, got1[half].at[slot(sign)], near[axis][sign])
        for sign in (1, -1):
            src = rp.at[strip(half, vs[sign], quarter(half, -sign), 256)]
            dst = got2[half].at[slot(sign), slot(-sign)]
            alone1[half, sign] = put(src, dst, near[axis][sign])

    def sum_second(half):
        axis, _, vs, _ = scatter[half]
        for sign in (1, -1):
            sums1[half, sign].wait_recv()
            at = strip(half, vs[sign], quarter(half, sign), 256)
            rp[at] = (f32(rp[at]) + f32(got1[half][slot(sign)])).astype(jnp.bfloat16)
            dst = got2[half].at[slot(sign), slot(sign)]
            sums2[half, sign] = put(rp.at[at], dst, near[axis][sign])

    def line_sum(half, u, i):
        at = (*one(half, u), pl.ds(half * 512 + i * 256, 256))
        got = got2[half]
        if half == 0:
            a, b = got[0, i, u // 2, u % 2], got[1, i, u // 2, u % 2]
        else:
            a, b = got[0, i, u], got[1, i, u]
        rp[at] = (f32(rp[at]) + f32(a) + f32(b)).astype(jnp.bfloat16)
        return rp.at[at]

    def sum_third(half):
        _, axis, _, us = scatter[half]
        for sign in (1, -1):
            alone1[half, sign].wait_recv()
        for sign in (1, -1):
            sums2[half, sign].wait_recv()
        for sign in (1, -1):
            src = line_sum(half, us[2], slot(sign))
            last1[half, sign] = put(src, rc1.at[half, slot(sign)], near[axis][sign])
        for sign in (1, -1):
            src = line_sum(half, us[sign], slot(-sign))
            alone2[half, sign] = put(src, rc2.at[half, slot(sign), slot(-sign)], near[axis][sign])
        for sign in (1, -1):
            line_sum(half, us[sign], slot(sign))
            line_sum(half, us[0], slot(sign))

    def sum_fourth(half):
        _, axis, _, us = scatter[half]
        for sign in (1, -1):
            last1[half, sign].wait_recv()
            at = (*one(half, us[sign]), pl.ds(quarter(half, sign), 256))
            rp[at] = (f32(rp[at]) + f32(rc1[half, slot(sign)])).astype(jnp.bfloat16)
            dst = rc2.at[half, slot(sign), slot(sign)]
            last2[half, sign] = put(rp.at[at], dst, near[axis][sign])

    def sum_last(half):
        _, _, _, us = scatter[half]
        for sign in (1, -1):
            alone2[half, sign].wait_recv()
        for sign in (1, -1):
            last2[half, sign].wait_recv()
        for i in (0, 1):
            rows = pl.ds(half * 512 + i * 256, 256)
            mine = f32(rp[(*one(half, us[0]), rows)])
            fin[rows, :] = (mine + f32(rc2[half, 0, i]) + f32(rc2[half, 1, i])).astype(jnp.bfloat16)
        rows = pl.ds(half * 512, 512)
        back[half] = put(fin.at[rows], fin_in.at[rows], partner, swapped)

    def give(half):
        def write(result):
            for p in range(half * 4, half * 4 + 4):
                rows = slice(p * 128, p * 128 + 128)
                out_ref[rows, :] = (f32(result[rows, :]) * mask(p)).astype(jnp.bfloat16)

        @pl.when(swapped)
        def _():
            back[half].wait_recv()
            write(fin_in)

        pl.when(home)(lambda: write(fin))

    own_start(0)
    own_start(1)
    own_here(0)
    t_send(1)
    plane_own()
    own_here(1)
    f_send(1, 0)
    a_start(0)
    a_x(0)
    b_start(0)
    a_start(1)
    b_y(0)
    t_step(1)
    b_start(1)
    b_y2(0)
    f_send(1, 1)
    t_step(2)
    a_x(1)
    b_y(1)
    a_y(1, 0)
    f_step(1, 0)
    side_send("t", 0)
    a_x2(1)
    b_x(0, 1)
    t_step(3)
    b_x(0, 3)
    b_x(0, 2)
    a_x2(0)
    f_step(1, 1)
    a_y(1, 1)
    f_step(2, 0)
    b_y2(1)
    a_y(0, 0)
    t_step(4)
    b_x(0, 0)
    b_x(1, 1)
    side_send("f", 0)
    a_y(0, 1)
    b_x(1, 2)
    b_x(1, 0)
    f_step(2, 1)
    t_done()
    b_done(0)
    stage1(8)
    b_x(1, 3)
    a_done(1)
    stage1(4)
    a_done(0)
    stage1(0)
    b_done(1)
    stage1(12)
    f_step(3, 0)
    f_step(3, 1)
    stage2(3, 5)
    stage2(0, 3)
    f_step(4, 0)
    f_step(4, 1)
    stage2(5, 7)
    stage2(7, 8)

    def both(step):
        step(0)
        step(1)

    both(sum_first)
    both(sum_second)
    both(sum_third)
    both(sum_fourth)
    both(sum_last)
    both(give)

    @pl.when(swapped)
    def _():
        for far, _ in moves:
            far.wait_send()

    for condition, copy in pending:
        when(condition, copy.wait_send)


def ladder(virt, occ, pair, t, ft, f):
    bf16 = jnp.bfloat16
    hbm, vmem = pl.BlockSpec(memory_space=pl.ANY), pl.BlockSpec(memory_space=pltpu.VMEM)
    smem = pl.BlockSpec(memory_space=pltpu.SMEM)
    return pl.pallas_call(
        kernel,
        out_shape=jax.ShapeDtypeStruct((1024, 128), bf16),
        in_specs=[smem, smem, smem, vmem, hbm, hbm],
        out_specs=vmem,
        scratch_shapes=[
            pltpu.VMEM((128, 1024), bf16),
            pltpu.VMEM((16, 128, 1024), bf16),
            pltpu.VMEM((16, 16, 128, 128), bf16),
            pltpu.VMEM((2, 4, 2, 16, 128, 128), bf16),
            pltpu.VMEM((1024, 2048), bf16),
            pltpu.VMEM((2, 4, 2, 1024, 128), bf16),
            pltpu.VMEM((2, 2, 2, 256, 128), bf16),
            pltpu.VMEM((2, 2, 2, 2, 256, 128), bf16),
            pltpu.VMEM((2, 4, 256, 128), bf16),
            pltpu.VMEM((2, 2, 4, 256, 128), bf16),
            pltpu.VMEM((2, 2, 256, 128), bf16),
            pltpu.VMEM((2, 2, 2, 256, 128), bf16),
            pltpu.VMEM((1024, 128), bf16),
            pltpu.VMEM((1024, 128), bf16),
            pltpu.SemaphoreType.DMA((N_SEMS,)),
            pltpu.SemaphoreType.DMA((N_SEMS,)),
        ],
        compiler_params=pltpu.CompilerParams(
            collective_id=0, has_side_effects=True, vmem_limit_bytes=56 * 1024 * 1024
        ),
    )(virt, occ, pair, t, ft, f)


def on_device(amplitudes, factors, virt_irrep, occupied_symmetry_label, pair_index):
    rows, pairs, width = amplitudes.shape
    t = amplitudes.transpose(2, 1, 0).reshape(width, pairs * rows)
    ft = factors.transpose(0, 2, 1)
    pair = pair_index.reshape(pairs * 2)
    out = ladder(virt_irrep, occupied_symmetry_label, pair, t, ft, factors)
    return out.reshape(pairs, width, rows).transpose(2, 0, 1)


def solution(mesh):
    in_specs = (P("row", None, "col"), P(None, "row", "col"), P(), P(), P())
    out_specs = P("row", None, "col")
    return jax.shard_map(
        on_device, mesh=mesh, in_specs=in_specs, out_specs=out_specs, check_vma=False
    )
```

```python
import jax
import jax.numpy as jnp
from jax import lax
from jax.experimental import pallas as pl
from jax.experimental.pallas import tpu as pltpu
from jax.sharding import PartitionSpec as P

VB = 64
MESH = pl.DeviceIdType.MESH
N_SEMS = 190


def kernel(
    virt, occ, pair, t_ref, ft_ref, f_ref, out_ref,
    t_own, t_all, fca, fdb, ht, rp, ra1, ra2, rb1, rb2, rc1, rc2, own_in,
    send, recv,
):
    row, col = lax.axis_index("row"), lax.axis_index("col")
    xh, y, k = row // 8, (row // 2) % 4, row % 2
    xl, z = col // 8, col % 8
    x = xh * 2 + xl

    def dev(x_to, y_to, z_to, k_to):
        return {"row": (x_to // 2) * 8 + y_to * 2 + k_to, "col": (x_to % 2) * 8 + z_to}

    def wrap(v, n):
        return lax.rem(v + n, n)

    xs = {s: wrap(x + s, 4) for s in (-1, 0, 1, 2)}
    ys = {s: wrap(y + s, 4) for s in (-1, 0, 1, 2)}
    zs = {s: wrap(z + s, 8) for s in range(-4, 5)}
    near = {
        "x": {s: dev(xs[s], y, z, k) for s in (-1, 1)},
        "y": {s: dev(x, ys[s], z, k) for s in (-1, 1)},
        "z": {s: dev(x, y, zs[s], k) for s in (-1, 1)},
    }
    sibling = dev(x, y, z, 1 - k)
    partner = dev(xh * 2 + k, y, z, xl)
    swapped = xl != k
    home = xl == k
    owner = {
        "x": {s: dev((xs[s] // 2) * 2 + k, y, z, xs[s] % 2) for s in (-1, 1)},
        "y": {s: dev(xh * 2 + k, ys[s], z, xl) for s in (-1, 1)},
    }
    across_chip = dev(xs[2], y, z, 1 - k)

    count = [0]
    pending = []

    def when(condition, action):
        if condition is None:
            action()
        else:
            pl.when(condition)(action)

    def put(src, dst, device, condition=None):
        number = count[0]
        count[0] += 1
        copy = pltpu.make_async_remote_copy(
            src_ref=src, dst_ref=dst, send_sem=send.at[number], recv_sem=recv.at[number],
            device_id=device, device_id_type=MESH,
        )
        when(condition, copy.start)
        pending.append((condition, copy))
        return copy

    def sign_of(label):
        return (1 - 2 * lax.rem(label, 2)).astype(jnp.float32)

    def two(block):
        low = lax.broadcasted_iota(jnp.int32, (1, 128), 1) < VB
        return jnp.where(low, sign_of(virt[2 * block]), sign_of(virt[2 * block + 1]))

    def two_rows(block):
        low = lax.broadcasted_iota(jnp.int32, (128, 1), 0) < VB
        return jnp.where(low, sign_of(virt[2 * block]), sign_of(virt[2 * block + 1]))

    pair_sign = [sign_of(occ[pair[p, 0]] + occ[pair[p, 1]]) for p in range(8)]

    def mask(p):
        return 0.5 + 0.5 * (two_rows(col) * (two(row) * pair_sign[p]))

    barrier = pltpu.get_barrier_semaphore()
    for target in [*near["x"].values(), *near["y"].values(), *near["z"].values(), sibling, across_chip]:
        pl.semaphore_signal(barrier, inc=1, device_id=target, device_id_type=MESH)

    for p in range(8):
        at = slice(p * 128, p * 128 + 128)
        t_own[:, at] = (t_ref[:, at].astype(jnp.float32) * mask(p)).astype(jnp.bfloat16)

    @pl.when(swapped)
    def _():
        for target in [partner, *owner["y"].values()]:
            pl.semaphore_signal(barrier, inc=1, device_id=target, device_id_type=MESH)
        pl.semaphore_wait(barrier, 11)

    @pl.when(jnp.logical_not(swapped))
    def _():
        pl.semaphore_wait(barrier, 8)

    moves = []
    for src, dst in ((t_own, t_all.at[col]), (f_ref, fca.at[col])):
        number = count[0]
        count[0] += 1
        far = pltpu.make_async_remote_copy(
            src_ref=src, dst_ref=dst, send_sem=send.at[number], recv_sem=recv.at[number],
            device_id=partner, device_id_type=MESH,
        )
        near_copy = pltpu.make_async_copy(src, dst, recv.at[number])
        moves.append((far, near_copy))

    def own_start(i):
        far, near_copy = moves[i]

        @pl.when(swapped)
        def _():
            far.start()

        @pl.when(jnp.logical_not(swapped))
        def _():
            near_copy.start()

    def own_here(i):
        far, near_copy = moves[i]

        @pl.when(swapped)
        def _():
            far.wait_recv()

        @pl.when(jnp.logical_not(swapped))
        def _():
            near_copy.wait()

    ring_wait = {}
    side_wait = {}

    def part(name, shard, half):
        buf = t_all if name == "t" else fca
        at = k * 8 + shard
        rows = buf.shape[1]
        if half is None:
            return buf.at[at]
        return buf.at[at, pl.ds(half * (rows // 2), rows // 2)]

    def side_send(name, step):
        for sign in (1, -1) if step % 4 else (1,):
            piece = part(name, zs[-sign * step], None)
            side_wait[name, step, sign] = put(piece, piece, sibling)

    def side_done(name, step):
        for sign in (1, -1) if step % 4 else (1,):
            side_wait[name, step, sign].wait_recv()

    def t_send(step):
        for sign in (1, -1):
            piece = part("t", zs[-sign * (step - 1)], None if step < 4 else (1 - sign) // 2)
            ring_wait["t", step, sign] = put(piece, piece, near["z"][sign])

    def t_step(step):
        for sign in (1, -1):
            ring_wait["t", step, sign].wait_recv()
        if step < 4:
            t_send(step + 1)
        side_send("t", step)

    def t_done():
        for step in range(5):
            side_done("t", step)

    def f_send(step, half):
        for sign in (1, -1):
            if step < 4 or half == (1 - sign) // 2:
                piece = part("f", zs[-sign * (step - 1)], half)
                ring_wait["f", step, sign, half] = put(piece, piece, near["z"][sign])

    def f_step(step, half):
        for sign in (1, -1):
            if step < 4 or half == (1 - sign) // 2:
                ring_wait["f", step, sign, half].wait_recv()
        if step < 4:
            f_send(step + 1, half)
        if half == 1:
            side_send("f", step)

    def unit(xh_of, y_of, start, size):
        return fdb.at[xh_of, y_of, :, pl.ds(start, size)]

    def both_ways(piece, axis, condition=None):
        return {sign: put(piece, piece, near[axis][sign], condition) for sign in (1, -1)}

    lines = [jnp.where(home, xh, xs[-1] // 2), jnp.where(home, 1 - xh, xs[1] // 2)]
    sides = {1: xs[-1] // 2, -1: xs[1] // 2}
    moved = {}

    def wait(key, condition=None):
        for sign in (1, -1):
            when(condition, moved[key][sign].wait_recv)

    def a_start(s):
        own = unit(xh, y, 4 * s, 4)
        moved["ax", s] = both_ways(own, "x", home)

    def a_along(s, i, condition=None):
        piece = unit(lines[i], y, 4 * s, 4)
        return both_ways(piece, "y", condition)

    def b_start(s):
        own = unit(xh, y, 8 + 4 * s, 4)
        moved["by", s] = both_ways(own, "y", home)
        b_along(s, 0)

    def b_along(s, j):
        piece = unit(xh, ys[(0, -1, 1, 2)[j]], 8 + 4 * s, 4)
        moved["bx", s, j] = both_ways(piece, "x", home)

    def a_x(s):
        wait(("ax", s), swapped)
        moved["ax2", s] = {
            sign: put(piece, piece, near["x"][sign], swapped)
            for sign in (1, -1)
            for piece in [unit(sides[sign], y, 4 * s + 1 - sign, 2)]
        }
        moved["ay", s, 0] = a_along(s, 0)

    def a_x2(s):
        wait(("ax2", s), home)
        moved["ay", s, 1] = a_along(s, 1)

    def a_y(s, i):
        wait(("ay", s, i))
        moved["ay2", s, i] = {
            sign: put(piece, piece, near["y"][sign])
            for sign in (1, -1)
            for piece in [unit(lines[i], ys[-sign], 4 * s + 1 - sign, 2)]
        }

    def b_y(s):
        wait(("by", s), home)
        moved["by2", s] = {
            sign: put(piece, piece, near["y"][sign], home)
            for sign in (1, -1)
            for piece in [unit(xh, ys[-sign], 8 + 4 * s + 1 - sign, 2)]
        }
        b_along(s, 1)
        b_along(s, 2)

    def b_y2(s):
        wait(("by2", s), home)
        b_along(s, 3)

    def b_x(s, j):
        wait(("bx", s, j), swapped)
        moved["bx2", s, j] = {
            sign: put(piece, piece, near["x"][sign], swapped)
            for sign in (1, -1)
            for piece in [unit(sides[sign], ys[(0, -1, 1, 2)[j]], 8 + 4 * s + 1 - sign, 2)]
        }

    def a_done(s):
        for i in (0, 1):
            wait(("ay2", s, i))

    def b_done(s):
        for j in range(4):
            wait(("bx2", s, j), home)

    given = put(ft_ref, fdb.at[xh, y, k], sibling, swapped)
    kept = pltpu.make_async_copy(ft_ref, fdb.at[xh, y, k], send.at[N_SEMS - 1])
    pl.when(home)(kept.start)

    def plane_own():
        pl.when(home)(given.wait_recv)
        pl.when(home)(kept.wait)

    def stage1(first_q):
        def body(n, _):
            lhs = jnp.concatenate(
                [
                    fdb[r // 8, (r // 2) % 4, r % 2, first_q : first_q + 4].reshape(512, 128)
                    for r in range(16)
                ],
                axis=1,
            )
            rhs = t_all[:, :, pl.ds(pl.multiple_of(n * 256, 256), 256)].reshape(2048, 256)
            out = jnp.dot(lhs, rhs, preferred_element_type=jnp.float32).astype(jnp.bfloat16)
            for i in range(2):
                rows = pl.ds(pl.multiple_of(n * 256 + i * 128, 128), 128)
                for j in range(4):
                    at = (first_q + j) * 128
                    ht[rows, at : at + 128] = out[j * 128 : j * 128 + 128, i * 128 : i * 128 + 128]
            return 0

        lax.fori_loop(0, 4, body, 0)

    def stage2(lo, hi):
        for step in sorted({(n + 1) // 2 for n in range(lo, hi)}):
            side_done("f", step)

        def body(n, _):
            away = (n + 1) // 2
            shard = wrap(z + jnp.where(lax.rem(n, 2) == 1, away, 8 - away), 8)
            rhs = jnp.concatenate(
                [fca[shard].reshape(2048, 128), fca[8 + shard].reshape(2048, 128)], axis=1
            )
            out = jnp.dot(ht[...], rhs, preferred_element_type=jnp.float32).astype(jnp.bfloat16)
            rp[0, shard // 2, lax.rem(shard, 2)] = out[:, :128]
            rp[1, shard // 2, lax.rem(shard, 2)] = out[:, 128:]
            return 0

        lax.fori_loop(lo, hi, body, 0)

    def strip(half, v, start, size):
        if half == 0:
            return (slice(None), v, slice(None), pl.ds(start, size))
        return (v // 2, slice(None), v % 2, pl.ds(start, size))

    sums1, sums2, last1, last2, alone1, alone2, back = {}, {}, {}, {}, {}, {}, {}
    got1, got2 = {0: ra1, 1: rb1}, {0: ra2, 1: rb2}

    def slot(sign):
        return (1 - sign) // 2

    def quarter(half, sign):
        return half * 512 + slot(sign) * 256

    def one(half, u):
        return (u // 2, y, u % 2) if half == 0 else (x // 2, u, x % 2)

    def f32(v):
        return v.astype(jnp.float32)

    odd = lax.rem(z, 2) == 1
    group_y = [wrap(z // 2 + jnp.where(odd, s, (-s) % 4), 4) for s in (0, 1, 3, 2)]

    def later(src, dst, device):
        number = count[0]
        count[0] += 1
        copy = pltpu.make_async_remote_copy(
            src_ref=src, dst_ref=dst, send_sem=send.at[number], recv_sem=recv.at[number],
            device_id=device, device_id_type=MESH,
        )
        pending.append((None, copy))
        return copy

    for sign in (1, -1):
        src = rp.at[strip(0, ys[2], quarter(0, sign), 256)]
        sums1[0, sign] = later(src, ra1.at[slot(sign)], near["y"][sign])
        src = rp.at[strip(0, ys[sign], quarter(0, -sign), 256)]
        alone1[0, sign] = later(src, ra2.at[slot(sign), slot(-sign)], near["y"][sign])
        src = rp.at[(*one(1, ys[2]), pl.ds(quarter(1, sign), 256))]
        last1[1, sign] = later(src, rc1.at[1, slot(sign)], near["y"][sign])
        src = rp.at[(*one(1, ys[sign]), pl.ds(quarter(1, -sign), 256))]
        alone2[1, sign] = later(src, rc2.at[1, slot(sign), slot(-sign)], owner["y"][sign])

    def by_part(g, far, next_to):
        away = wrap(group_y[g] - y, 4)

        @pl.when(away == 2)
        def _():
            far[1].start()
            far[-1].start()

        pl.when(away == 1)(next_to[1].start)
        pl.when(away == 3)(next_to[-1].start)

    def group_send(g):
        by_part(g, {s: sums1[0, s] for s in (1, -1)}, {s: alone1[0, s] for s in (1, -1)})
        for sign in (1, -1):
            src = rp.at[xs[2] // 2, group_y[g], xs[2] % 2, pl.ds(quarter(1, sign), 256)]
            sums1[1, g, sign] = put(src, rb1.at[slot(sign), group_y[g]], near["x"][sign])
        for sign in (1, -1):
            src = rp.at[xs[sign] // 2, group_y[g], xs[sign] % 2, pl.ds(quarter(1, -sign), 256)]
            dst = rb2.at[slot(sign), slot(-sign), group_y[g]]
            alone1[1, g, sign] = put(src, dst, near["x"][sign])

    def b_sum(g):
        for sign in (1, -1):
            sums1[1, g, sign].wait_recv()
            at = (xs[sign] // 2, group_y[g], xs[sign] % 2, pl.ds(quarter(1, sign), 256))
            rp[at] = (f32(rp[at]) + f32(rb1[slot(sign), group_y[g]])).astype(jnp.bfloat16)
            dst = rb2.at[slot(sign), slot(sign), group_y[g]]
            sums2[1, g, sign] = put(rp.at[at], dst, near["x"][sign])

    def line_sum(half, u, i):
        at = (*one(half, u), pl.ds(half * 512 + i * 256, 256))
        got = got2[half]
        if half == 0:
            a, b = got[0, i, u // 2, u % 2], got[1, i, u // 2, u % 2]
        else:
            a, b = got[0, i, u], got[1, i, u]
        rp[at] = (f32(rp[at]) + f32(a) + f32(b)).astype(jnp.bfloat16)
        return rp.at[at]

    def b_line(g):
        for sign in (1, -1):
            alone1[1, g, sign].wait_recv()
            sums2[1, g, sign].wait_recv()
        for i in (0, 1):
            line_sum(1, group_y[g], i)
        by_part(g, {s: last1[1, s] for s in (1, -1)}, {s: alone2[1, s] for s in (1, -1)})

    def a_sum():
        for sign in (1, -1):
            sums1[0, sign].wait_recv()
            at = strip(0, ys[sign], quarter(0, sign), 256)
            rp[at] = (f32(rp[at]) + f32(ra1[slot(sign)])).astype(jnp.bfloat16)
            sums2[0, sign] = put(rp.at[at], ra2.at[slot(sign), slot(sign)], near["y"][sign])

    def a_line():
        for sign in (1, -1):
            alone1[0, sign].wait_recv()
            sums2[0, sign].wait_recv()
        for sign in (1, -1):
            src = line_sum(0, xs[2], slot(sign))
            last1[0, sign] = put(src, rc1.at[0, slot(sign)], near["x"][sign])
        for sign in (1, -1):
            src = line_sum(0, xs[sign], slot(-sign))
            alone2[0, sign] = put(src, rc2.at[0, slot(sign), slot(-sign)], owner["x"][sign])
        for sign in (1, -1):
            line_sum(0, xs[0], slot(sign))
        own_send(0)
        for sign in (1, -1):
            line_sum(0, xs[sign], slot(sign))

    def sum_fourth(half):
        axis, us = (("x", xs), ("y", ys))[half]
        for sign in (1, -1):
            last1[half, sign].wait_recv()
            at = (*one(half, us[sign]), pl.ds(quarter(half, sign), 256))
            rp[at] = (f32(rp[at]) + f32(rc1[half, slot(sign)])).astype(jnp.bfloat16)
            dst = rc2.at[half, slot(sign), slot(sign)]
            last2[half, sign] = put(rp.at[at], dst, owner[axis][sign])

    def own_send(half):
        rows = pl.ds(half * 512, 512)
        back[half] = put(rp.at[x // 2, y, x % 2, rows], own_in.at[rows], partner, swapped)

    def sum_last(half):
        for sign in (1, -1):
            alone2[half, sign].wait_recv()
            last2[half, sign].wait_recv()

        def write(own):
            for p in range(half * 4, half * 4 + 4):
                rows = slice(p * 128, p * 128 + 128)
                i, got = (p % 4) // 2, slice((p % 2) * 128, (p % 2) * 128 + 128)
                total = f32(own(rows)) + f32(rc2[half, 0, i, got]) + f32(rc2[half, 1, i, got])
                out_ref[rows, :] = (total * mask(p)).astype(jnp.bfloat16)

        @pl.when(swapped)
        def _():
            back[half].wait_recv()
            write(lambda rows: own_in[rows, :])

        pl.when(home)(lambda: write(lambda rows: rp[x // 2, y, x % 2, rows, :]))

    own_start(0)
    own_here(0)
    t_send(1)
    plane_own()
    own_start(1)
    t_step(1)
    a_start(1)
    b_start(1)
    own_here(1)
    a_x(1)
    f_send(1, 0)
    b_y(1)
    a_y(1, 0)
    b_start(0)
    f_send(1, 1)
    side_send("t", 0)
    t_step(2)
    b_y2(1)
    f_step(1, 0)
    a_x2(1)
    side_send("f", 0)
    a_start(0)
    b_x(1, 3)
    a_x(0)
    t_step(3)
    b_y(0)
    b_y2(0)
    b_x(1, 1)
    a_y(1, 1)
    f_step(1, 1)
    b_x(1, 2)
    a_y(0, 0)
    f_step(2, 0)
    a_done(1)
    b_x(0, 1)
    t_step(4)
    t_done()
    a_x2(0)
    b_x(1, 0)
    b_x(0, 2)
    stage1(4)
    b_x(0, 0)
    b_x(0, 3)
    f_step(2, 1)
    b_done(1)
    stage1(12)
    b_done(0)
    a_y(0, 1)
    stage1(8)
    a_done(0)
    f_step(3, 0)
    f_step(3, 1)
    stage1(0)
    stage2(0, 3)
    group_send(0)
    stage2(3, 5)
    group_send(1)
    b_sum(0)
    f_step(4, 0)
    f_step(4, 1)
    stage2(5, 7)
    group_send(2)
    b_sum(1)
    stage2(7, 8)
    group_send(3)
    b_sum(2)
    b_line(0)
    b_sum(3)
    b_line(1)
    b_line(2)
    a_sum()
    b_line(3)
    own_send(1)
    a_line()
    sum_fourth(1)
    sum_fourth(0)
    sum_last(1)
    sum_last(0)

    @pl.when(swapped)
    def _():
        for far, _ in moves:
            far.wait_send()

    for condition, copy in pending:
        when(condition, copy.wait_send)


def ladder(virt, occ, pair, t, ft, f):
    bf16 = jnp.bfloat16
    hbm, vmem = pl.BlockSpec(memory_space=pl.ANY), pl.BlockSpec(memory_space=pltpu.VMEM)
    smem = pl.BlockSpec(memory_space=pltpu.SMEM)
    return pl.pallas_call(
        kernel,
        out_shape=jax.ShapeDtypeStruct((1024, 128), bf16),
        in_specs=[smem, smem, smem, vmem, hbm, hbm],
        out_specs=vmem,
        scratch_shapes=[
            pltpu.VMEM((128, 1024), bf16),
            pltpu.VMEM((16, 128, 1024), bf16),
            pltpu.VMEM((16, 16, 128, 128), bf16),
            pltpu.VMEM((2, 4, 2, 16, 128, 128), bf16),
            pltpu.VMEM((1024, 2048), bf16),
            pltpu.VMEM((2, 4, 2, 1024, 128), bf16),
            pltpu.VMEM((2, 2, 2, 256, 128), bf16),
            pltpu.VMEM((2, 2, 2, 2, 256, 128), bf16),
            pltpu.VMEM((2, 4, 256, 128), bf16),
            pltpu.VMEM((2, 2, 4, 256, 128), bf16),
            pltpu.VMEM((2, 2, 256, 128), bf16),
            pltpu.VMEM((2, 2, 2, 256, 128), bf16),
            pltpu.VMEM((1024, 128), bf16),
            pltpu.SemaphoreType.DMA((N_SEMS,)),
            pltpu.SemaphoreType.DMA((N_SEMS,)),
        ],
        compiler_params=pltpu.CompilerParams(
            collective_id=0, has_side_effects=True, vmem_limit_bytes=56 * 1024 * 1024
        ),
    )(virt, occ, pair, t, ft, f)


def on_device(amplitudes, factors, virt_irrep, occupied_symmetry_label, pair_index):
    rows, pairs, width = amplitudes.shape
    t = amplitudes.transpose(2, 1, 0).reshape(width, pairs * rows)
    ft = factors.transpose(0, 2, 1)
    out = ladder(virt_irrep, occupied_symmetry_label, pair_index, t, ft, factors)
    return out.reshape(pairs, width, rows).transpose(2, 0, 1)


def solution(mesh):
    in_specs = (P("row", None, "col"), P(None, "row", "col"), P(), P(), P())
    out_specs = P("row", None, "col")
    return jax.shard_map(
        on_device, mesh=mesh, in_specs=in_specs, out_specs=out_specs, check_vma=False
    )
```

```python
import jax
import jax.numpy as jnp
from jax import lax
from jax.experimental import pallas as pl
from jax.experimental.pallas import tpu as pltpu
from jax.sharding import PartitionSpec as P

VB = 64
MESH = pl.DeviceIdType.MESH
N_SEMS = 190


def kernel(
    virt, occ, pair, t_ref, ft_ref, f_ref, out_ref,
    t_own, t_all, fca, fdb, ht, rp, ra1, ra2, rb1, rb2, rc1, rc2, own_in,
    send, recv,
):
    row, col = lax.axis_index("row"), lax.axis_index("col")
    xh, y, k = row // 8, (row // 2) % 4, row % 2
    xl, z = col // 8, col % 8
    x = xh * 2 + xl

    def dev(x_to, y_to, z_to, k_to):
        return {"row": (x_to // 2) * 8 + y_to * 2 + k_to, "col": (x_to % 2) * 8 + z_to}

    def wrap(v, n):
        return lax.rem(v + n, n)

    xs = {s: wrap(x + s, 4) for s in (-1, 0, 1, 2)}
    ys = {s: wrap(y + s, 4) for s in (-1, 0, 1, 2)}
    zs = {s: wrap(z + s, 8) for s in range(-4, 5)}
    near = {
        "x": {s: dev(xs[s], y, z, k) for s in (-1, 1)},
        "y": {s: dev(x, ys[s], z, k) for s in (-1, 1)},
        "z": {s: dev(x, y, zs[s], k) for s in (-1, 1)},
    }
    sibling = dev(x, y, z, 1 - k)
    partner = dev(xh * 2 + k, y, z, xl)
    swapped = xl != k
    home = xl == k
    owner = {
        "x": {s: dev((xs[s] // 2) * 2 + k, y, z, xs[s] % 2) for s in (-1, 1)},
        "y": {s: dev(xh * 2 + k, ys[s], z, xl) for s in (-1, 1)},
    }
    across_chip = dev(xs[2], y, z, 1 - k)

    count = [0]
    pending = []

    def when(condition, action):
        if condition is None:
            action()
        else:
            pl.when(condition)(action)

    def put(src, dst, device, condition=None):
        number = count[0]
        count[0] += 1
        copy = pltpu.make_async_remote_copy(
            src_ref=src, dst_ref=dst, send_sem=send.at[number], recv_sem=recv.at[number],
            device_id=device, device_id_type=MESH,
        )
        when(condition, copy.start)
        pending.append((condition, copy))
        return copy

    def sign_of(label):
        return (1 - 2 * lax.rem(label, 2)).astype(jnp.float32)

    def two(block):
        low = lax.broadcasted_iota(jnp.int32, (1, 128), 1) < VB
        return jnp.where(low, sign_of(virt[2 * block]), sign_of(virt[2 * block + 1]))

    def two_rows(block):
        low = lax.broadcasted_iota(jnp.int32, (128, 1), 0) < VB
        return jnp.where(low, sign_of(virt[2 * block]), sign_of(virt[2 * block + 1]))

    pair_sign = [sign_of(occ[pair[0, p]] + occ[pair[1, p]]) for p in range(8)]

    def mask(p):
        return 0.5 + 0.5 * (two_rows(col) * (two(row) * pair_sign[p]))

    barrier = pltpu.get_barrier_semaphore()
    for target in [*near["x"].values(), *near["y"].values(), *near["z"].values(), sibling, across_chip]:
        pl.semaphore_signal(barrier, inc=1, device_id=target, device_id_type=MESH)

    for p in range(8):
        at = slice(p * 128, p * 128 + 128)
        t_own[:, at] = (t_ref[:, p, :].astype(jnp.float32) * mask(p)).astype(jnp.bfloat16)

    @pl.when(swapped)
    def _():
        for target in [partner, *owner["y"].values()]:
            pl.semaphore_signal(barrier, inc=1, device_id=target, device_id_type=MESH)
        pl.semaphore_wait(barrier, 11)

    @pl.when(jnp.logical_not(swapped))
    def _():
        pl.semaphore_wait(barrier, 8)

    moves = []
    for src, dst in ((t_own, t_all.at[col]), (f_ref, fca.at[col])):
        number = count[0]
        count[0] += 1
        far = pltpu.make_async_remote_copy(
            src_ref=src, dst_ref=dst, send_sem=send.at[number], recv_sem=recv.at[number],
            device_id=partner, device_id_type=MESH,
        )
        near_copy = pltpu.make_async_copy(src, dst, recv.at[number])
        moves.append((far, near_copy))

    def own_start(i):
        far, near_copy = moves[i]

        @pl.when(swapped)
        def _():
            far.start()

        @pl.when(jnp.logical_not(swapped))
        def _():
            near_copy.start()

    def own_here(i):
        far, near_copy = moves[i]

        @pl.when(swapped)
        def _():
            far.wait_recv()

        @pl.when(jnp.logical_not(swapped))
        def _():
            near_copy.wait()

    ring_wait = {}
    side_wait = {}

    def part(name, shard, half):
        buf = t_all if name == "t" else fca
        at = k * 8 + shard
        rows = buf.shape[1]
        if half is None:
            return buf.at[at]
        return buf.at[at, pl.ds(half * (rows // 2), rows // 2)]

    def side_send(name, step):
        for sign in (1, -1) if step % 4 else (1,):
            piece = part(name, zs[-sign * step], None)
            side_wait[name, step, sign] = put(piece, piece, sibling)

    def side_done(name, step):
        for sign in (1, -1) if step % 4 else (1,):
            side_wait[name, step, sign].wait_recv()

    def t_send(step):
        for sign in (1, -1):
            piece = part("t", zs[-sign * (step - 1)], None if step < 4 else (1 - sign) // 2)
            ring_wait["t", step, sign] = put(piece, piece, near["z"][sign])

    def t_step(step):
        for sign in (1, -1):
            ring_wait["t", step, sign].wait_recv()
        if step < 4:
            t_send(step + 1)
        side_send("t", step)

    def t_done():
        for step in range(5):
            side_done("t", step)

    def f_send(step, half):
        for sign in (1, -1):
            if step < 4 or half == (1 - sign) // 2:
                piece = part("f", zs[-sign * (step - 1)], half)
                ring_wait["f", step, sign, half] = put(piece, piece, near["z"][sign])

    def f_step(step, half):
        for sign in (1, -1):
            if step < 4 or half == (1 - sign) // 2:
                ring_wait["f", step, sign, half].wait_recv()
        if step < 4:
            f_send(step + 1, half)
        if half == 1:
            side_send("f", step)

    def unit(xh_of, y_of, start, size):
        return fdb.at[xh_of, y_of, :, pl.ds(start, size)]

    def both_ways(piece, axis, condition=None):
        return {sign: put(piece, piece, near[axis][sign], condition) for sign in (1, -1)}

    lines = [jnp.where(home, xh, xs[-1] // 2), jnp.where(home, 1 - xh, xs[1] // 2)]
    sides = {1: xs[-1] // 2, -1: xs[1] // 2}
    moved = {}

    def wait(key, condition=None):
        for sign in (1, -1):
            when(condition, moved[key][sign].wait_recv)

    def a_start(s):
        own = unit(xh, y, 4 * s, 4)
        moved["ax", s] = both_ways(own, "x", home)

    def a_along(s, i, condition=None):
        piece = unit(lines[i], y, 4 * s, 4)
        return both_ways(piece, "y", condition)

    def b_start(s):
        own = unit(xh, y, 8 + 4 * s, 4)
        moved["by", s] = both_ways(own, "y", home)
        b_along(s, 0)

    def b_along(s, j):
        piece = unit(xh, ys[(0, -1, 1, 2)[j]], 8 + 4 * s, 4)
        moved["bx", s, j] = both_ways(piece, "x", home)

    def a_x(s):
        wait(("ax", s), swapped)
        moved["ax2", s] = {
            sign: put(piece, piece, near["x"][sign], swapped)
            for sign in (1, -1)
            for piece in [unit(sides[sign], y, 4 * s + 1 - sign, 2)]
        }
        moved["ay", s, 0] = a_along(s, 0)

    def a_x2(s):
        wait(("ax2", s), home)
        moved["ay", s, 1] = a_along(s, 1)

    def a_y(s, i):
        wait(("ay", s, i))
        moved["ay2", s, i] = {
            sign: put(piece, piece, near["y"][sign])
            for sign in (1, -1)
            for piece in [unit(lines[i], ys[-sign], 4 * s + 1 - sign, 2)]
        }

    def b_y(s):
        wait(("by", s), home)
        moved["by2", s] = {
            sign: put(piece, piece, near["y"][sign], home)
            for sign in (1, -1)
            for piece in [unit(xh, ys[-sign], 8 + 4 * s + 1 - sign, 2)]
        }
        b_along(s, 1)
        b_along(s, 2)

    def b_y2(s):
        wait(("by2", s), home)
        b_along(s, 3)

    def b_x(s, j):
        wait(("bx", s, j), swapped)
        moved["bx2", s, j] = {
            sign: put(piece, piece, near["x"][sign], swapped)
            for sign in (1, -1)
            for piece in [unit(sides[sign], ys[(0, -1, 1, 2)[j]], 8 + 4 * s + 1 - sign, 2)]
        }

    def a_done(s):
        for i in (0, 1):
            wait(("ay2", s, i))

    def b_done(s):
        for j in range(4):
            wait(("bx2", s, j), home)

    given = put(ft_ref, fdb.at[xh, y, k], sibling, swapped)
    kept = pltpu.make_async_copy(ft_ref, fdb.at[xh, y, k], send.at[N_SEMS - 1])
    pl.when(home)(kept.start)

    def plane_own():
        pl.when(home)(given.wait_recv)
        pl.when(home)(kept.wait)

    def stage1(first_q):
        def body(n, _):
            lhs = jnp.concatenate(
                [
                    fdb[r // 8, (r // 2) % 4, r % 2, first_q : first_q + 4].reshape(512, 128)
                    for r in range(16)
                ],
                axis=1,
            )
            rhs = t_all[:, :, pl.ds(pl.multiple_of(n * 256, 256), 256)].reshape(2048, 256)
            out = jnp.dot(lhs, rhs, preferred_element_type=jnp.float32).astype(jnp.bfloat16)
            for i in range(2):
                rows = pl.ds(pl.multiple_of(n * 256 + i * 128, 128), 128)
                for j in range(4):
                    at = (first_q + j) * 128
                    ht[rows, at : at + 128] = out[j * 128 : j * 128 + 128, i * 128 : i * 128 + 128]
            return 0

        lax.fori_loop(0, 4, body, 0)

    def stage2(lo, hi):
        for step in sorted({(n + 1) // 2 for n in range(lo, hi)}):
            side_done("f", step)

        def body(n, _):
            away = (n + 1) // 2
            shard = wrap(z + jnp.where(lax.rem(n, 2) == 1, away, 8 - away), 8)
            rhs = jnp.concatenate(
                [fca[shard].reshape(2048, 128), fca[8 + shard].reshape(2048, 128)], axis=1
            )
            out = jnp.dot(ht[...], rhs, preferred_element_type=jnp.float32).astype(jnp.bfloat16)
            rp[0, shard // 2, lax.rem(shard, 2)] = out[:, :128]
            rp[1, shard // 2, lax.rem(shard, 2)] = out[:, 128:]
            return 0

        lax.fori_loop(lo, hi, body, 0)

    def strip(half, v, start, size):
        if half == 0:
            return (slice(None), v, slice(None), pl.ds(start, size))
        return (v // 2, slice(None), v % 2, pl.ds(start, size))

    sums1, sums2, last1, last2, alone1, alone2, back = {}, {}, {}, {}, {}, {}, {}
    got1, got2 = {0: ra1, 1: rb1}, {0: ra2, 1: rb2}

    def slot(sign):
        return (1 - sign) // 2

    def quarter(half, sign):
        return half * 512 + slot(sign) * 256

    def one(half, u):
        return (u // 2, y, u % 2) if half == 0 else (x // 2, u, x % 2)

    def f32(v):
        return v.astype(jnp.float32)

    odd = lax.rem(z, 2) == 1
    group_y = [wrap(z // 2 + jnp.where(odd, s, (-s) % 4), 4) for s in (0, 1, 3, 2)]

    def later(src, dst, device):
        number = count[0]
        count[0] += 1
        copy = pltpu.make_async_remote_copy(
            src_ref=src, dst_ref=dst, send_sem=send.at[number], recv_sem=recv.at[number],
            device_id=device, device_id_type=MESH,
        )
        pending.append((None, copy))
        return copy

    for sign in (1, -1):
        src = rp.at[strip(0, ys[2], quarter(0, sign), 256)]
        sums1[0, sign] = later(src, ra1.at[slot(sign)], near["y"][sign])
        src = rp.at[strip(0, ys[sign], quarter(0, -sign), 256)]
        alone1[0, sign] = later(src, ra2.at[slot(sign), slot(-sign)], near["y"][sign])
        src = rp.at[(*one(1, ys[2]), pl.ds(quarter(1, sign), 256))]
        last1[1, sign] = later(src, rc1.at[1, slot(sign)], near["y"][sign])
        src = rp.at[(*one(1, ys[sign]), pl.ds(quarter(1, -sign), 256))]
        alone2[1, sign] = later(src, rc2.at[1, slot(sign), slot(-sign)], owner["y"][sign])

    def by_part(g, far, next_to):
        away = wrap(group_y[g] - y, 4)

        @pl.when(away == 2)
        def _():
            far[1].start()
            far[-1].start()

        pl.when(away == 1)(next_to[1].start)
        pl.when(away == 3)(next_to[-1].start)

    def group_send(g):
        by_part(g, {s: sums1[0, s] for s in (1, -1)}, {s: alone1[0, s] for s in (1, -1)})
        for sign in (1, -1):
            src = rp.at[xs[2] // 2, group_y[g], xs[2] % 2, pl.ds(quarter(1, sign), 256)]
            sums1[1, g, sign] = put(src, rb1.at[slot(sign), group_y[g]], near["x"][sign])
        for sign in (1, -1):
            src = rp.at[xs[sign] // 2, group_y[g], xs[sign] % 2, pl.ds(quarter(1, -sign), 256)]
            dst = rb2.at[slot(sign), slot(-sign), group_y[g]]
            alone1[1, g, sign] = put(src, dst, near["x"][sign])

    def b_sum(g):
        for sign in (1, -1):
            sums1[1, g, sign].wait_recv()
            at = (xs[sign] // 2, group_y[g], xs[sign] % 2, pl.ds(quarter(1, sign), 256))
            rp[at] = (f32(rp[at]) + f32(rb1[slot(sign), group_y[g]])).astype(jnp.bfloat16)
            dst = rb2.at[slot(sign), slot(sign), group_y[g]]
            sums2[1, g, sign] = put(rp.at[at], dst, near["x"][sign])

    def line_sum(half, u, i):
        at = (*one(half, u), pl.ds(half * 512 + i * 256, 256))
        got = got2[half]
        if half == 0:
            a, b = got[0, i, u // 2, u % 2], got[1, i, u // 2, u % 2]
        else:
            a, b = got[0, i, u], got[1, i, u]
        rp[at] = (f32(rp[at]) + f32(a) + f32(b)).astype(jnp.bfloat16)
        return rp.at[at]

    def b_line(g):
        for sign in (1, -1):
            alone1[1, g, sign].wait_recv()
            sums2[1, g, sign].wait_recv()
        for i in (0, 1):
            line_sum(1, group_y[g], i)
        by_part(g, {s: last1[1, s] for s in (1, -1)}, {s: alone2[1, s] for s in (1, -1)})

    def a_sum():
        for sign in (1, -1):
            sums1[0, sign].wait_recv()
            at = strip(0, ys[sign], quarter(0, sign), 256)
            rp[at] = (f32(rp[at]) + f32(ra1[slot(sign)])).astype(jnp.bfloat16)
            sums2[0, sign] = put(rp.at[at], ra2.at[slot(sign), slot(sign)], near["y"][sign])

    def a_line():
        for sign in (1, -1):
            alone1[0, sign].wait_recv()
            sums2[0, sign].wait_recv()
        for sign in (1, -1):
            src = line_sum(0, xs[2], slot(sign))
            last1[0, sign] = put(src, rc1.at[0, slot(sign)], near["x"][sign])
        for sign in (1, -1):
            src = line_sum(0, xs[sign], slot(-sign))
            alone2[0, sign] = put(src, rc2.at[0, slot(sign), slot(-sign)], owner["x"][sign])
        for sign in (1, -1):
            line_sum(0, xs[0], slot(sign))
        own_send(0)
        for sign in (1, -1):
            line_sum(0, xs[sign], slot(sign))

    def sum_fourth(half):
        axis, us = (("x", xs), ("y", ys))[half]
        for sign in (1, -1):
            last1[half, sign].wait_recv()
            at = (*one(half, us[sign]), pl.ds(quarter(half, sign), 256))
            rp[at] = (f32(rp[at]) + f32(rc1[half, slot(sign)])).astype(jnp.bfloat16)
            dst = rc2.at[half, slot(sign), slot(sign)]
            last2[half, sign] = put(rp.at[at], dst, owner[axis][sign])

    def own_send(half):
        rows = pl.ds(half * 512, 512)
        back[half] = put(rp.at[x // 2, y, x % 2, rows], own_in.at[rows], partner, swapped)

    def sum_last(half):
        for sign in (1, -1):
            alone2[half, sign].wait_recv()
            last2[half, sign].wait_recv()

        def write(own):
            for p in range(half * 4, half * 4 + 4):
                rows = slice(p * 128, p * 128 + 128)
                i, got = (p % 4) // 2, slice((p % 2) * 128, (p % 2) * 128 + 128)
                total = f32(own(rows)) + f32(rc2[half, 0, i, got]) + f32(rc2[half, 1, i, got])
                out_ref[rows, :] = (total * mask(p)).astype(jnp.bfloat16)

        @pl.when(swapped)
        def _():
            back[half].wait_recv()
            write(lambda rows: own_in[rows, :])

        pl.when(home)(lambda: write(lambda rows: rp[x // 2, y, x % 2, rows, :]))

    own_start(0)
    own_here(0)
    t_send(1)
    plane_own()
    own_start(1)
    t_step(1)
    a_start(1)
    b_start(1)
    own_here(1)
    a_x(1)
    f_send(1, 0)
    b_y(1)
    a_y(1, 0)
    b_start(0)
    f_send(1, 1)
    side_send("t", 0)
    t_step(2)
    b_y2(1)
    f_step(1, 0)
    a_x2(1)
    side_send("f", 0)
    a_start(0)
    b_x(1, 3)
    a_x(0)
    t_step(3)
    b_y(0)
    b_y2(0)
    b_x(1, 1)
    a_y(1, 1)
    f_step(1, 1)
    b_x(1, 2)
    a_y(0, 0)
    f_step(2, 0)
    a_done(1)
    b_x(0, 1)
    t_step(4)
    t_done()
    a_x2(0)
    b_x(1, 0)
    b_x(0, 2)
    stage1(4)
    b_x(0, 0)
    b_x(0, 3)
    f_step(2, 1)
    b_done(1)
    stage1(12)
    b_done(0)
    a_y(0, 1)
    stage1(8)
    a_done(0)
    f_step(3, 0)
    f_step(3, 1)
    stage1(0)
    stage2(0, 3)
    group_send(0)
    stage2(3, 5)
    group_send(1)
    b_sum(0)
    f_step(4, 0)
    f_step(4, 1)
    stage2(5, 7)
    group_send(2)
    b_sum(1)
    stage2(7, 8)
    group_send(3)
    b_sum(2)
    b_line(0)
    b_sum(3)
    b_line(1)
    b_line(2)
    a_sum()
    b_line(3)
    own_send(1)
    a_line()
    sum_fourth(1)
    sum_fourth(0)
    sum_last(1)
    sum_last(0)

    @pl.when(swapped)
    def _():
        for far, _ in moves:
            far.wait_send()

    for condition, copy in pending:
        when(condition, copy.wait_send)


def ladder(virt, occ, pair, t, ft, f):
    bf16 = jnp.bfloat16
    hbm, vmem = pl.BlockSpec(memory_space=pl.ANY), pl.BlockSpec(memory_space=pltpu.VMEM)
    smem = pl.BlockSpec(memory_space=pltpu.SMEM)
    return pl.pallas_call(
        kernel,
        out_shape=jax.ShapeDtypeStruct((1024, 128), bf16),
        in_specs=[smem, smem, smem, vmem, hbm, hbm],
        out_specs=vmem,
        scratch_shapes=[
            pltpu.VMEM((128, 1024), bf16),
            pltpu.VMEM((16, 128, 1024), bf16),
            pltpu.VMEM((16, 16, 128, 128), bf16),
            pltpu.VMEM((2, 4, 2, 16, 128, 128), bf16),
            pltpu.VMEM((1024, 2048), bf16),
            pltpu.VMEM((2, 4, 2, 1024, 128), bf16),
            pltpu.VMEM((2, 2, 2, 256, 128), bf16),
            pltpu.VMEM((2, 2, 2, 2, 256, 128), bf16),
            pltpu.VMEM((2, 4, 256, 128), bf16),
            pltpu.VMEM((2, 2, 4, 256, 128), bf16),
            pltpu.VMEM((2, 2, 256, 128), bf16),
            pltpu.VMEM((2, 2, 2, 256, 128), bf16),
            pltpu.VMEM((1024, 128), bf16),
            pltpu.SemaphoreType.DMA((N_SEMS,)),
            pltpu.SemaphoreType.DMA((N_SEMS,)),
        ],
        compiler_params=pltpu.CompilerParams(
            collective_id=0, has_side_effects=True, vmem_limit_bytes=56 * 1024 * 1024
        ),
    )(virt, occ, pair, t, ft, f)


def on_device(amplitudes, factors, virt_irrep, occupied_symmetry_label, pair_index):
    rows, pairs, width = amplitudes.shape
    t = amplitudes.transpose(2, 1, 0)
    ft = factors.transpose(0, 2, 1)
    out = ladder(virt_irrep, occupied_symmetry_label, pair_index.T, t, ft, factors)
    return out.reshape(pairs, width, rows).transpose(2, 0, 1)


def solution(mesh):
    in_specs = (P("row", None, "col"), P(None, "row", "col"), P(), P(), P())
    out_specs = P("row", None, "col")
    return jax.shard_map(
        on_device, mesh=mesh, in_specs=in_specs, out_specs=out_specs, check_vma=False
    )
```

```python
import jax
import jax.numpy as jnp
from jax import lax
from jax.experimental import pallas as pl
from jax.experimental.pallas import tpu as pltpu
from jax.sharding import PartitionSpec as P

VB = 64
MESH = pl.DeviceIdType.MESH
N_SEMS = 190


def kernel(
    virt, occ, pair, t_ref, f_ref, out_ref,
    t_own, f_own, ft_own, t_all, fca, fdb, ht, rp, ra1, ra2, rb1, rb2, rc1, rc2, own_in,
    send, recv,
):
    row, col = lax.axis_index("row"), lax.axis_index("col")
    xh, y, k = row // 8, (row // 2) % 4, row % 2
    xl, z = col // 8, col % 8
    x = xh * 2 + xl

    def dev(x_to, y_to, z_to, k_to):
        return {"row": (x_to // 2) * 8 + y_to * 2 + k_to, "col": (x_to % 2) * 8 + z_to}

    def wrap(v, n):
        return lax.rem(v + n, n)

    xs = {s: wrap(x + s, 4) for s in (-1, 0, 1, 2)}
    ys = {s: wrap(y + s, 4) for s in (-1, 0, 1, 2)}
    zs = {s: wrap(z + s, 8) for s in range(-4, 5)}
    near = {
        "x": {s: dev(xs[s], y, z, k) for s in (-1, 1)},
        "y": {s: dev(x, ys[s], z, k) for s in (-1, 1)},
        "z": {s: dev(x, y, zs[s], k) for s in (-1, 1)},
    }
    sibling = dev(x, y, z, 1 - k)
    partner = dev(xh * 2 + k, y, z, xl)
    swapped = xl != k
    home = xl == k
    owner = {
        "x": {s: dev((xs[s] // 2) * 2 + k, y, z, xs[s] % 2) for s in (-1, 1)},
        "y": {s: dev(xh * 2 + k, ys[s], z, xl) for s in (-1, 1)},
    }
    across_chip = dev(xs[2], y, z, 1 - k)

    count = [0]
    pending = []

    def when(condition, action):
        if condition is None:
            action()
        else:
            pl.when(condition)(action)

    def put(src, dst, device, condition=None):
        number = count[0]
        count[0] += 1
        copy = pltpu.make_async_remote_copy(
            src_ref=src, dst_ref=dst, send_sem=send.at[number], recv_sem=recv.at[number],
            device_id=device, device_id_type=MESH,
        )
        when(condition, copy.start)
        pending.append((condition, copy))
        return copy

    def sign_of(label):
        return (1 - 2 * lax.rem(label, 2)).astype(jnp.float32)

    def two(block):
        low = lax.broadcasted_iota(jnp.int32, (1, 128), 1) < VB
        return jnp.where(low, sign_of(virt[2 * block]), sign_of(virt[2 * block + 1]))

    def two_rows(block):
        low = lax.broadcasted_iota(jnp.int32, (128, 1), 0) < VB
        return jnp.where(low, sign_of(virt[2 * block]), sign_of(virt[2 * block + 1]))

    pair_sign = [sign_of(occ[pair[0, p]] + occ[pair[1, p]]) for p in range(8)]

    def mask(p):
        return 0.5 + 0.5 * (two_rows(col) * (two(row) * pair_sign[p]))

    fetched = pltpu.make_async_copy(f_ref, f_own, send.at[N_SEMS - 2])
    fetched.start()

    barrier = pltpu.get_barrier_semaphore()
    for target in [*near["x"].values(), *near["y"].values(), *near["z"].values(), sibling, across_chip]:
        pl.semaphore_signal(barrier, inc=1, device_id=target, device_id_type=MESH)

    for p in range(8):
        at = slice(p * 128, p * 128 + 128)
        t_own[:, at] = (t_ref[:, p, :].astype(jnp.float32) * mask(p)).astype(jnp.bfloat16)

    @pl.when(swapped)
    def _():
        for target in [partner, *owner["y"].values()]:
            pl.semaphore_signal(barrier, inc=1, device_id=target, device_id_type=MESH)
        pl.semaphore_wait(barrier, 11)

    @pl.when(jnp.logical_not(swapped))
    def _():
        pl.semaphore_wait(barrier, 8)

    moves = []
    for src, dst in ((t_own, t_all.at[col]), (f_ref, fca.at[col])):
        number = count[0]
        count[0] += 1
        far = pltpu.make_async_remote_copy(
            src_ref=src, dst_ref=dst, send_sem=send.at[number], recv_sem=recv.at[number],
            device_id=partner, device_id_type=MESH,
        )
        near_copy = pltpu.make_async_copy(src, dst, recv.at[number])
        moves.append((far, near_copy))

    def own_start(i):
        far, near_copy = moves[i]

        @pl.when(swapped)
        def _():
            far.start()

        @pl.when(jnp.logical_not(swapped))
        def _():
            near_copy.start()

    def own_here(i):
        far, near_copy = moves[i]

        @pl.when(swapped)
        def _():
            far.wait_recv()

        @pl.when(jnp.logical_not(swapped))
        def _():
            near_copy.wait()

    ring_wait = {}
    side_wait = {}

    def part(name, shard, half):
        buf = t_all if name == "t" else fca
        at = k * 8 + shard
        rows = buf.shape[1]
        if half is None:
            return buf.at[at]
        return buf.at[at, pl.ds(half * (rows // 2), rows // 2)]

    def side_send(name, step):
        for sign in (1, -1) if step % 4 else (1,):
            piece = part(name, zs[-sign * step], None)
            side_wait[name, step, sign] = put(piece, piece, sibling)

    def side_done(name, step):
        for sign in (1, -1) if step % 4 else (1,):
            side_wait[name, step, sign].wait_recv()

    def t_send(step):
        for sign in (1, -1):
            piece = part("t", zs[-sign * (step - 1)], None if step < 4 else (1 - sign) // 2)
            ring_wait["t", step, sign] = put(piece, piece, near["z"][sign])

    def t_step(step):
        for sign in (1, -1):
            ring_wait["t", step, sign].wait_recv()
        if step < 4:
            t_send(step + 1)
        side_send("t", step)

    def t_done():
        for step in range(5):
            side_done("t", step)

    def f_send(step, half):
        for sign in (1, -1):
            if step < 4 or half == (1 - sign) // 2:
                piece = part("f", zs[-sign * (step - 1)], half)
                ring_wait["f", step, sign, half] = put(piece, piece, near["z"][sign])

    def f_step(step, half):
        for sign in (1, -1):
            if step < 4 or half == (1 - sign) // 2:
                ring_wait["f", step, sign, half].wait_recv()
        if step < 4:
            f_send(step + 1, half)
        if half == 1:
            side_send("f", step)

    def unit(xh_of, y_of, start, size):
        return fdb.at[xh_of, y_of, :, pl.ds(start, size)]

    def both_ways(piece, axis, condition=None):
        return {sign: put(piece, piece, near[axis][sign], condition) for sign in (1, -1)}

    lines = [jnp.where(home, xh, xs[-1] // 2), jnp.where(home, 1 - xh, xs[1] // 2)]
    sides = {1: xs[-1] // 2, -1: xs[1] // 2}
    moved = {}

    def wait(key, condition=None):
        for sign in (1, -1):
            when(condition, moved[key][sign].wait_recv)

    def a_start(s):
        own = unit(xh, y, 4 * s, 4)
        moved["ax", s] = both_ways(own, "x", home)

    def a_along(s, i, condition=None):
        piece = unit(lines[i], y, 4 * s, 4)
        return both_ways(piece, "y", condition)

    def b_start(s):
        own = unit(xh, y, 8 + 4 * s, 4)
        moved["by", s] = both_ways(own, "y", home)
        b_along(s, 0)

    def b_along(s, j):
        piece = unit(xh, ys[(0, -1, 1, 2)[j]], 8 + 4 * s, 4)
        moved["bx", s, j] = both_ways(piece, "x", home)

    def a_x(s):
        wait(("ax", s), swapped)
        moved["ax2", s] = {
            sign: put(piece, piece, near["x"][sign], swapped)
            for sign in (1, -1)
            for piece in [unit(sides[sign], y, 4 * s + 1 - sign, 2)]
        }
        moved["ay", s, 0] = a_along(s, 0)

    def a_x2(s):
        wait(("ax2", s), home)
        moved["ay", s, 1] = a_along(s, 1)

    def a_y(s, i):
        wait(("ay", s, i))
        moved["ay2", s, i] = {
            sign: put(piece, piece, near["y"][sign])
            for sign in (1, -1)
            for piece in [unit(lines[i], ys[-sign], 4 * s + 1 - sign, 2)]
        }

    def b_y(s):
        wait(("by", s), home)
        moved["by2", s] = {
            sign: put(piece, piece, near["y"][sign], home)
            for sign in (1, -1)
            for piece in [unit(xh, ys[-sign], 8 + 4 * s + 1 - sign, 2)]
        }
        b_along(s, 1)
        b_along(s, 2)

    def b_y2(s):
        wait(("by2", s), home)
        b_along(s, 3)

    def b_x(s, j):
        wait(("bx", s, j), swapped)
        moved["bx2", s, j] = {
            sign: put(piece, piece, near["x"][sign], swapped)
            for sign in (1, -1)
            for piece in [unit(sides[sign], ys[(0, -1, 1, 2)[j]], 8 + 4 * s + 1 - sign, 2)]
        }

    def a_done(s):
        for i in (0, 1):
            wait(("ay2", s, i))

    def b_done(s):
        for j in range(4):
            wait(("bx2", s, j), home)

    def plane_own():
        pl.when(home)(given.wait_recv)
        pl.when(home)(kept.wait)

    def stage1(first_q):
        def body(n, _):
            lhs = jnp.concatenate(
                [
                    fdb[r // 8, (r // 2) % 4, r % 2, first_q : first_q + 4].reshape(512, 128)
                    for r in range(16)
                ],
                axis=1,
            )
            rhs = t_all[:, :, pl.ds(pl.multiple_of(n * 256, 256), 256)].reshape(2048, 256)
            out = jnp.dot(lhs, rhs, preferred_element_type=jnp.float32).astype(jnp.bfloat16)
            for i in range(2):
                rows = pl.ds(pl.multiple_of(n * 256 + i * 128, 128), 128)
                for j in range(4):
                    at = (first_q + j) * 128
                    ht[rows, at : at + 128] = out[j * 128 : j * 128 + 128, i * 128 : i * 128 + 128]
            return 0

        lax.fori_loop(0, 4, body, 0)

    def stage2(lo, hi):
        for step in sorted({(n + 1) // 2 for n in range(lo, hi)}):
            side_done("f", step)

        def body(n, _):
            away = (n + 1) // 2
            shard = wrap(z + jnp.where(lax.rem(n, 2) == 1, away, 8 - away), 8)
            rhs = jnp.concatenate(
                [fca[shard].reshape(2048, 128), fca[8 + shard].reshape(2048, 128)], axis=1
            )
            out = jnp.dot(ht[...], rhs, preferred_element_type=jnp.float32).astype(jnp.bfloat16)
            rp[0, shard // 2, lax.rem(shard, 2)] = out[:, :128]
            rp[1, shard // 2, lax.rem(shard, 2)] = out[:, 128:]
            return 0

        lax.fori_loop(lo, hi, body, 0)

    def strip(half, v, start, size):
        if half == 0:
            return (slice(None), v, slice(None), pl.ds(start, size))
        return (v // 2, slice(None), v % 2, pl.ds(start, size))

    sums1, sums2, last1, last2, alone1, alone2, back = {}, {}, {}, {}, {}, {}, {}
    got1, got2 = {0: ra1, 1: rb1}, {0: ra2, 1: rb2}

    def slot(sign):
        return (1 - sign) // 2

    def quarter(half, sign):
        return half * 512 + slot(sign) * 256

    def one(half, u):
        return (u // 2, y, u % 2) if half == 0 else (x // 2, u, x % 2)

    def f32(v):
        return v.astype(jnp.float32)

    odd = lax.rem(z, 2) == 1
    group_y = [wrap(z // 2 + jnp.where(odd, s, (-s) % 4), 4) for s in (0, 1, 3, 2)]

    def later(src, dst, device):
        number = count[0]
        count[0] += 1
        copy = pltpu.make_async_remote_copy(
            src_ref=src, dst_ref=dst, send_sem=send.at[number], recv_sem=recv.at[number],
            device_id=device, device_id_type=MESH,
        )
        pending.append((None, copy))
        return copy

    for sign in (1, -1):
        src = rp.at[strip(0, ys[2], quarter(0, sign), 256)]
        sums1[0, sign] = later(src, ra1.at[slot(sign)], near["y"][sign])
        src = rp.at[strip(0, ys[sign], quarter(0, -sign), 256)]
        alone1[0, sign] = later(src, ra2.at[slot(sign), slot(-sign)], near["y"][sign])
        src = rp.at[(*one(1, ys[2]), pl.ds(quarter(1, sign), 256))]
        last1[1, sign] = later(src, rc1.at[1, slot(sign)], near["y"][sign])
        src = rp.at[(*one(1, ys[sign]), pl.ds(quarter(1, -sign), 256))]
        alone2[1, sign] = later(src, rc2.at[1, slot(sign), slot(-sign)], owner["y"][sign])

    def by_part(g, far, next_to):
        away = wrap(group_y[g] - y, 4)

        @pl.when(away == 2)
        def _():
            far[1].start()
            far[-1].start()

        pl.when(away == 1)(next_to[1].start)
        pl.when(away == 3)(next_to[-1].start)

    def group_send(g):
        by_part(g, {s: sums1[0, s] for s in (1, -1)}, {s: alone1[0, s] for s in (1, -1)})
        for sign in (1, -1):
            src = rp.at[xs[2] // 2, group_y[g], xs[2] % 2, pl.ds(quarter(1, sign), 256)]
            sums1[1, g, sign] = put(src, rb1.at[slot(sign), group_y[g]], near["x"][sign])
        for sign in (1, -1):
            src = rp.at[xs[sign] // 2, group_y[g], xs[sign] % 2, pl.ds(quarter(1, -sign), 256)]
            dst = rb2.at[slot(sign), slot(-sign), group_y[g]]
            alone1[1, g, sign] = put(src, dst, near["x"][sign])

    def b_sum(g):
        for sign in (1, -1):
            sums1[1, g, sign].wait_recv()
            at = (xs[sign] // 2, group_y[g], xs[sign] % 2, pl.ds(quarter(1, sign), 256))
            rp[at] = (f32(rp[at]) + f32(rb1[slot(sign), group_y[g]])).astype(jnp.bfloat16)
            dst = rb2.at[slot(sign), slot(sign), group_y[g]]
            sums2[1, g, sign] = put(rp.at[at], dst, near["x"][sign])

    def line_sum(half, u, i):
        at = (*one(half, u), pl.ds(half * 512 + i * 256, 256))
        got = got2[half]
        if half == 0:
            a, b = got[0, i, u // 2, u % 2], got[1, i, u // 2, u % 2]
        else:
            a, b = got[0, i, u], got[1, i, u]
        rp[at] = (f32(rp[at]) + f32(a) + f32(b)).astype(jnp.bfloat16)
        return rp.at[at]

    def b_line(g):
        for sign in (1, -1):
            alone1[1, g, sign].wait_recv()
            sums2[1, g, sign].wait_recv()
        for i in (0, 1):
            line_sum(1, group_y[g], i)
        by_part(g, {s: last1[1, s] for s in (1, -1)}, {s: alone2[1, s] for s in (1, -1)})

    def a_sum():
        for sign in (1, -1):
            sums1[0, sign].wait_recv()
            at = strip(0, ys[sign], quarter(0, sign), 256)
            rp[at] = (f32(rp[at]) + f32(ra1[slot(sign)])).astype(jnp.bfloat16)
            sums2[0, sign] = put(rp.at[at], ra2.at[slot(sign), slot(sign)], near["y"][sign])

    def a_line():
        for sign in (1, -1):
            alone1[0, sign].wait_recv()
            sums2[0, sign].wait_recv()
        for sign in (1, -1):
            src = line_sum(0, xs[2], slot(sign))
            last1[0, sign] = put(src, rc1.at[0, slot(sign)], near["x"][sign])
        for sign in (1, -1):
            src = line_sum(0, xs[sign], slot(-sign))
            alone2[0, sign] = put(src, rc2.at[0, slot(sign), slot(-sign)], owner["x"][sign])
        for sign in (1, -1):
            line_sum(0, xs[0], slot(sign))
        own_send(0)
        for sign in (1, -1):
            line_sum(0, xs[sign], slot(sign))

    def sum_fourth(half):
        axis, us = (("x", xs), ("y", ys))[half]
        for sign in (1, -1):
            last1[half, sign].wait_recv()
            at = (*one(half, us[sign]), pl.ds(quarter(half, sign), 256))
            rp[at] = (f32(rp[at]) + f32(rc1[half, slot(sign)])).astype(jnp.bfloat16)
            dst = rc2.at[half, slot(sign), slot(sign)]
            last2[half, sign] = put(rp.at[at], dst, owner[axis][sign])

    def own_send(half):
        rows = pl.ds(half * 512, 512)
        back[half] = put(rp.at[x // 2, y, x % 2, rows], own_in.at[rows], partner, swapped)

    def sum_last(half):
        for sign in (1, -1):
            alone2[half, sign].wait_recv()
            last2[half, sign].wait_recv()

        def write(own):
            for p in range(half * 4, half * 4 + 4):
                rows = slice(p * 128, p * 128 + 128)
                i, got = (p % 4) // 2, slice((p % 2) * 128, (p % 2) * 128 + 128)
                total = f32(own(rows)) + f32(rc2[half, 0, i, got]) + f32(rc2[half, 1, i, got])
                out_ref[rows, :] = (total * mask(p)).astype(jnp.bfloat16)

        @pl.when(swapped)
        def _():
            back[half].wait_recv()
            write(lambda rows: own_in[rows, :])

        pl.when(home)(lambda: write(lambda rows: rp[x // 2, y, x % 2, rows, :]))

    own_start(0)

    fetched.wait()

    @pl.loop(0, 16)
    def _(q):
        ft_own[q] = f_own[q].astype(jnp.float32).T.astype(jnp.bfloat16)

    given = put(ft_own, fdb.at[xh, y, k], sibling, swapped)
    kept = pltpu.make_async_copy(ft_own, fdb.at[xh, y, k], send.at[N_SEMS - 1])
    pl.when(home)(kept.start)

    own_here(0)
    t_send(1)
    plane_own()
    own_start(1)
    a_start(1)
    b_start(1)
    t_step(1)
    own_here(1)
    a_x(1)
    f_send(1, 0)
    b_y(1)
    a_y(1, 0)
    b_start(0)
    f_send(1, 1)
    side_send("t", 0)
    t_step(2)
    b_y2(1)
    f_step(1, 0)
    a_x2(1)
    side_send("f", 0)
    a_start(0)
    b_x(1, 3)
    a_x(0)
    t_step(3)
    b_y(0)
    b_y2(0)
    b_x(1, 1)
    a_y(1, 1)
    f_step(1, 1)
    b_x(1, 2)
    a_y(0, 0)
    f_step(2, 0)
    a_done(1)
    b_x(0, 1)
    t_step(4)
    t_done()
    a_x2(0)
    b_x(1, 0)
    b_x(0, 2)
    stage1(4)
    b_x(0, 0)
    b_x(0, 3)
    f_step(2, 1)
    b_done(1)
    stage1(12)
    b_done(0)
    a_y(0, 1)
    stage1(8)
    a_done(0)
    f_step(3, 0)
    f_step(3, 1)
    stage1(0)
    stage2(0, 3)
    group_send(0)
    stage2(3, 5)
    group_send(1)
    f_step(4, 0)
    f_step(4, 1)
    stage2(5, 7)
    group_send(2)
    b_sum(0)
    stage2(7, 8)
    group_send(3)
    b_sum(1)
    b_sum(2)
    b_line(0)
    b_sum(3)
    b_line(1)
    b_line(2)
    a_sum()
    b_line(3)
    own_send(1)
    a_line()
    sum_fourth(1)
    sum_fourth(0)
    sum_last(1)
    sum_last(0)

    @pl.when(swapped)
    def _():
        for far, _ in moves:
            far.wait_send()

    for condition, copy in pending:
        when(condition, copy.wait_send)


def ladder(virt, occ, pair, t, f):
    bf16 = jnp.bfloat16
    hbm, vmem = pl.BlockSpec(memory_space=pl.ANY), pl.BlockSpec(memory_space=pltpu.VMEM)
    smem = pl.BlockSpec(memory_space=pltpu.SMEM)
    return pl.pallas_call(
        kernel,
        out_shape=jax.ShapeDtypeStruct((1024, 128), bf16),
        in_specs=[smem, smem, smem, vmem, hbm],
        out_specs=vmem,
        scratch_shapes=[
            pltpu.VMEM((128, 1024), bf16),
            pltpu.VMEM((16, 128, 128), bf16),
            pltpu.VMEM((16, 128, 128), bf16),
            pltpu.VMEM((16, 128, 1024), bf16),
            pltpu.VMEM((16, 16, 128, 128), bf16),
            pltpu.VMEM((2, 4, 2, 16, 128, 128), bf16),
            pltpu.VMEM((1024, 2048), bf16),
            pltpu.VMEM((2, 4, 2, 1024, 128), bf16),
            pltpu.VMEM((2, 2, 2, 256, 128), bf16),
            pltpu.VMEM((2, 2, 2, 2, 256, 128), bf16),
            pltpu.VMEM((2, 4, 256, 128), bf16),
            pltpu.VMEM((2, 2, 4, 256, 128), bf16),
            pltpu.VMEM((2, 2, 256, 128), bf16),
            pltpu.VMEM((2, 2, 2, 256, 128), bf16),
            pltpu.VMEM((1024, 128), bf16),
            pltpu.SemaphoreType.DMA((N_SEMS,)),
            pltpu.SemaphoreType.DMA((N_SEMS,)),
        ],
        compiler_params=pltpu.CompilerParams(
            collective_id=0, has_side_effects=True, vmem_limit_bytes=56 * 1024 * 1024
        ),
    )(virt, occ, pair, t, f)


def on_device(amplitudes, factors, virt_irrep, occupied_symmetry_label, pair_index):
    rows, pairs, width = amplitudes.shape
    t = amplitudes.transpose(2, 1, 0)
    out = ladder(virt_irrep, occupied_symmetry_label, pair_index.T, t, factors)
    return out.reshape(pairs, width, rows).transpose(2, 0, 1)


def solution(mesh):
    in_specs = (P("row", None, "col"), P(None, "row", "col"), P(), P(), P())
    out_specs = P("row", None, "col")
    return jax.shard_map(
        on_device, mesh=mesh, in_specs=in_specs, out_specs=out_specs, check_vma=False
    )
```
